256 devices in a mesh: ta: 8 (over z_hi, core), gy: 4 (over x), gx: 8 (over y, z_lo).
Axes of the slice: x: 4, y: 4, z: 8 (z_hi: 4, z_lo: 2; z = z_hi * 2 + z_lo), core: 2. Of those that a mesh axis runs over, the one named last changes fastest.
Arguments:
- residual: bfloat16 [524288], P(('ta', 'gy', 'gx')), may hold values from -6 to 6
- footprint: bfloat16 [524288, 1024], P(('ta', 'gy', 'gx')), may hold values from 0.0099487305 to 1
- tile_id: int32 [524288, 1], P(('ta', 'gy', 'gx')), may hold values from 0 to 31; in each aligned block of 2048 rows (0 to 2047, 2048 to 4095, ...) at most 128 rows name the same one
- step_id: int32 [524288], P(('ta', 'gy', 'gx')), may hold values from 0 to 3
- block_id: int32 [524288], P(('ta', 'gy', 'gx')), may hold values from 0 to 15
- sigma: float32 [4, 256, 2048], P(None, 'gy', 'gx'), may hold values from 0.3 to 3
- taps: float32 [4, 5], replicated, may hold values from 0.05 to 0.4
- diffusivity: float32 [256, 2048], P('gy', 'gx'), may hold values from 0.03 to 0.24
Outputs:
- increment: float32 [4, 32, 256, 2048], P(None, 'ta', 'gy', 'gx')
The draws below stay inside these ranges and needn't reach their ends.
Inputs may be any that keep to these rules, and one draw needn't show every extreme that they name: `tile_id`: among the rows of one device at most 128 soundings name the same tile; some device reaches 128 in every draw. `block_id`: blocks are numbered row-major over 8 x 2 blocks of a tile.
All inputs are finite; a program needn't handle non-finite values.
Results may differ from the reference program's by a relative error of at most 0.006.
Values may be sent and summed in bfloat16 or wider, within the bound.
No kernel may reach another device: no remote copies, remote signals or barrier semaphores. Data moves between devices by JAX's collectives and lax.ppermute only.
A program may use at most 64 MiB of HBM per device.

```python
import math
import jax
import jax.numpy as jnp
import numpy as np
from jax import lax

TS_DEV = 4
SND_DEV = 2048
TRACERS = 4
BLK_LAT = 8
BLK_LON = 128
HB = 2
KSTEPS = 4
TAPS = 5
FP = 1024
NBR = 8
NBC = 2
BLOCKS = 16
CAP = 128
T_ALL = 32
NLAT = 256
NLON = 2048
SOUNDINGS = 524288
N_TA = 8
N_GY = 4
N_GX = 8


def place_ends(entries, stream_key, low, high):
    spot = [jax.random.randint(jax.random.fold_in(stream_key, axis), (), 0, length) for axis, length in enumerate(entries.shape)]
    widest = entries.shape.index(max(entries.shape))
    beside = spot[:widest] + [(spot[widest] + 1) % entries.shape[widest]] + spot[widest + 1:]
    return entries.at[tuple(spot)].set(low).at[tuple(beside)].set(high)


def level_of(rng, shape, shards, smallest, top_value):
    gain, own = 1.0, jax.random.fold_in(rng, 6)
    for dim, shards_of in shards:
        heights = jnp.exp(jax.random.uniform(jax.random.fold_in(own, dim), (shards_of,), jnp.float32, smallest / len(shards), top_value / len(shards)))
        gain = gain * jnp.repeat(heights, shape[dim] // shards_of).reshape([-1 if axis == dim else 1 for axis in range(len(shape))])
    return gain


def shared_out(rng, own, number, rows, number_of, top, bound, lean):
    sequence = jax.random.permutation(rng, number_of)
    crowded, usual = shares(number_of, rows * top, bound, lean, True), shares(number_of, rows * top, bound, lean, False)
    places = jnp.arange(number_of)

    def named(sizes, turn):
        used = int((sizes > 0).sum())
        fixed = max(1, used // 4)
        passed = fixed + (places - fixed + turn * (used - fixed)) % max(1, number_of - fixed)
        return jnp.zeros((number_of,), jnp.int32).at[sequence[jnp.where(places < fixed, places, passed)]].set(jnp.asarray(sizes, jnp.int32))

    sizes = jnp.where(number % 4 == 0, named(crowded, number // 4), named(usual, number - number // 4 - 1))
    mixed = jax.random.permutation(jax.random.fold_in(own, 3), number_of)
    giver, sink = mixed[0:number_of // 2 * 2:2], mixed[1:number_of // 2 * 2:2]
    margin = jnp.minimum(sizes[giver] - 1, bound - sizes[sink]) // 2
    margin = jnp.where((giver == sequence[0]) | (sink == sequence[0]) | (sizes[sink] == 0), 0, jnp.maximum(margin, 0))
    passed = jax.random.randint(jax.random.fold_in(own, 4), (number_of // 2,), 0, 1 << 20) % (margin + 1)
    sizes = sizes.at[giver].add(-passed).at[sink].add(passed)
    labels = jnp.searchsorted(jnp.cumsum(sizes), jnp.arange(rows * top), side="right").astype(jnp.int32)
    grid = labels.reshape(top, rows).T
    grid = grid[jax.random.permutation(jax.random.fold_in(own, 1), rows)]
    turn = jax.random.randint(jax.random.fold_in(own, 2), (rows, 1), 0, top)
    return jnp.take_along_axis(grid, (jnp.arange(top)[None, :] + turn) % top, axis=1)


def shares(amount, total, limit, slope, full):
    weights = [(1 << 20) // math.isqrt(grade ** slope) + 1 for grade in range(1, amount + 1)]
    largest = limit if full else min(limit, max(-(-total // amount), total * weights[0] // sum(weights)))
    least = 1 if total - largest >= amount - 1 else 0
    counts, rest = [largest] + [least] * (amount - 1), total - largest - least * (amount - 1)
    while rest > 0:
        free = [i for i in range(1, amount) if counts[i] < largest] or [i for i in range(1, amount) if counts[i] < limit]
        whole, remaining = sum([weights[i] for i in free]), rest
        for i in free:
            extra = min(limit - counts[i], max(1, remaining * weights[i] // whole), rest)
            counts[i] = counts[i] + extra
            rest = rest - extra
    return np.array(counts)


def noise(key, shape, width, limit, cuts=(), kind=jnp.bfloat16):
    factor_of = level_of(key, shape, cuts, -0.22, 0.18) if cuts else 1.0
    entries = jax.random.normal(key, shape, jnp.float32) * width * factor_of
    return jnp.minimum(jnp.maximum(entries, -limit), limit).astype(kind)


def setup_inputs(seed: int = 0) -> dict:
    key_list = jax.random.split(jax.random.key(seed), 9)
    residual = noise(key_list[0], (SOUNDINGS,), 1.0, 6.0, ((0, 256),))
    footprint = jnp.clip(jnp.exp(math.log(1.0) - 4.61031033 * jax.random.uniform(key_list[1], (SOUNDINGS, FP), jnp.float32) ** level_of(key_list[1], (SOUNDINGS, FP), ((0, 256),), -0.2, 0.2)), 0.0099487305, 1.0).astype(jnp.bfloat16)
    tile_id_keys = jax.random.split(jax.random.fold_in(key_list[2], 1), SOUNDINGS // SND_DEV)
    tile_id_turns = jax.random.permutation(jax.random.fold_in(key_list[2], 3), SOUNDINGS // SND_DEV)
    tile_id = jax.vmap(lambda own, number: shared_out(jax.random.fold_in(key_list[2], 2), own, number, SND_DEV, N_GY * N_GX, 1, CAP, 2))(tile_id_keys, tile_id_turns).reshape((SOUNDINGS, 1))
    step_id = place_ends(jax.random.randint(key_list[3], (SOUNDINGS,), 0, TS_DEV), jax.random.fold_in(key_list[3], 1), 0, TS_DEV - 1).astype(jnp.int32)
    block_id = place_ends(jax.random.randint(key_list[4], (SOUNDINGS,), 0, BLOCKS), jax.random.fold_in(key_list[4], 1), 0, BLOCKS - 1).astype(jnp.int32)
    sigma = jnp.clip(jnp.exp(math.log(3.0) - 2.3025851 * jax.random.uniform(key_list[5], (TRACERS, NLAT, NLON), jnp.float32) ** level_of(key_list[5], (TRACERS, NLAT, NLON), ((1, 4), (2, 8)), -0.2, 0.2)), 0.3, 3.0)
    taps = jnp.clip(jax.random.uniform(key_list[6], (TRACERS, TAPS), jnp.float32, 0.05, 0.4), 0.05, 0.4)
    diffusivity = jnp.clip(jnp.exp(math.log(0.24) - 2.0794415 * jax.random.uniform(key_list[7], (NLAT, NLON), jnp.float32) ** level_of(key_list[7], (NLAT, NLON), ((0, 4), (1, 8)), -0.2, 0.2)), 0.03, 0.24)
    return dict(residual=residual, footprint=footprint, tile_id=tile_id, step_id=step_id, block_id=block_id, sigma=sigma, taps=taps, diffusivity=diffusivity)


def build_adjoint(residual, footprint, tile_id, step_id, block_id):
    contrib = (residual.astype(jnp.float32)[:, None] * footprint.astype(jnp.float32)).astype(jnp.bfloat16)
    dest = tile_id[:, 0]
    row_blk = (dest // N_GX) * NBR + block_id // NBC
    col_blk = (dest % N_GX) * NBC + block_id % NBC
    segment = ((step_id * (N_GY * NBR) + row_blk) * (N_GX * NBC) + col_blk).astype(jnp.int32)
    local_bins = TS_DEV * N_GY * NBR * N_GX * NBC
    grouped_rows = contrib.reshape(N_TA, N_GY * N_GX, SND_DEV, FP)
    grouped_segs = segment.reshape(N_TA, N_GY * N_GX, SND_DEV)

    def one_slab(pair):
        def add_holder(total, item):
            part = jax.ops.segment_sum(item[0].astype(jnp.float32), item[1], num_segments=local_bins)
            rounded = lax.optimization_barrier(part.astype(jnp.bfloat16))
            return total + rounded.astype(jnp.float32), None

        total, unused = lax.scan(add_holder, jnp.zeros((local_bins, FP), jnp.float32), pair)
        return total

    summed = lax.map(one_slab, (grouped_rows, grouped_segs))
    summed = summed.reshape(T_ALL, N_GY * NBR, N_GX * NBC, BLK_LAT, BLK_LON)
    return summed.transpose(0, 1, 3, 2, 4).reshape(T_ALL, NLAT, NLON)


def reference(residual, footprint, tile_id, step_id, block_id, sigma, taps, diffusivity):
    adjoint = build_adjoint(residual, footprint, tile_id, step_id, block_id)
    padded = jnp.pad(adjoint, ((HB, HB), (0, 0), (0, 0)))
    banded = jnp.zeros((TRACERS, T_ALL, NLAT, NLON), jnp.float32)
    for offset in range(TAPS):
        banded = banded + taps[:, offset][:, None, None, None] * padded[None, offset:offset + T_ALL]
    field = sigma[:, None] * banded
    for sweep in range(KSTEPS):
        rows = jnp.pad(field, ((0, 0), (0, 0), (1, 1), (0, 0)))
        beside_all = rows[:, :, 2:] + rows[:, :, :-2] + jnp.roll(field, -1, axis=3) + jnp.roll(field, 1, axis=3)
        field = field + diffusivity * (beside_all - 4.0 * field)
    return sigma[:, None] * field
```

```python
import jax
import jax.numpy as jnp
from jax import lax
from jax.experimental import pallas as pl
from jax.experimental.pallas import tpu as pltpu
from jax.sharding import PartitionSpec as P

TS_DEV = 4
TRACERS = 4
HB = 2
KSTEPS = 4
LAT = 64
LON = 256
FP = 1024
BINS = 64
SND = 2048
TILES = 32
PAD_LAT = LAT + 16
PAD_LON = LON + 128
HALO = KSTEPS
F32 = jnp.float32
BF16 = jnp.bfloat16
MIB = 1 << 20


def vmem(*refs):
    return [pl.BlockSpec(memory_space=pltpu.VMEM)] * len(refs)


def bin_sums(bins, residual, footprint, col_blocks):
    cols = FP // col_blocks
    rows = 512

    def body(bins_ref, res_ref, fp_ref, out_ref, sel_ref):
        @pl.when(pl.program_id(0) == 0)
        def _():
            @pl.loop(0, TILES * BINS // 128)
            def _(m):
                first = m * 128
                number = lax.broadcasted_iota(jnp.int32, (128, SND), 0) + first
                hit = bins_ref[...] == number
                sel_ref[pl.ds(pl.multiple_of(first, 128), 128), :] = jnp.where(
                    hit, res_ref[...], 0.0
                ).astype(BF16)

        @pl.loop(0, TILES * BINS // rows)
        def _(m):
            at = pl.ds(pl.multiple_of(m * rows, rows), rows)
            out_ref[at, :] = jnp.dot(
                sel_ref[at, :], fp_ref[...], preferred_element_type=F32
            ).astype(BF16)

    return pl.pallas_call(
        body,
        grid=(col_blocks,),
        in_specs=[
            pl.BlockSpec((1, SND), lambda c: (0, 0)),
            pl.BlockSpec((1, SND), lambda c: (0, 0)),
            pl.BlockSpec((SND, cols), lambda c: (0, c)),
        ],
        out_specs=pl.BlockSpec((TILES * BINS, cols), lambda c: (0, c)),
        out_shape=jax.ShapeDtypeStruct((TILES * BINS, FP), BF16),
        scratch_shapes=[pltpu.VMEM((TILES * BINS, SND), BF16)],
        compiler_params=pltpu.CompilerParams(vmem_limit_bytes=40 * MIB),
        cost_estimate=pl.CostEstimate(
            flops=2 * TILES * BINS * SND * FP, bytes_accessed=8 * MIB, transcendentals=0
        ),
        name="bin_sums",
    )(bins, residual, footprint)


def tile_sum(got):
    def body(got_ref, adj_ref, send_ref, half_ref):
        total = got_ref[0].astype(F32)
        for s in range(1, TILES):
            total = total + got_ref[s].astype(F32)
        for bc in range(2):
            for i in range(8):
                half_ref[bc, pl.ds(i, 8, stride=8), :] = total[
                    bc * 8 : bc * 8 + 8, i * 128 : i * 128 + 128
                ]
            adj_ref[0, :, bc * 128 : bc * 128 + 128] = half_ref[bc]
        send_ref[...] = adj_ref[...].astype(BF16)

    return pl.pallas_call(
        body,
        grid=(TS_DEV,),
        in_specs=[pl.BlockSpec((TILES, BINS // TS_DEV, FP), lambda t: (0, t, 0))],
        out_specs=[pl.BlockSpec((1, LAT, LON), lambda t: (t, 0, 0))] * 2,
        out_shape=[
            jax.ShapeDtypeStruct((TS_DEV, LAT, LON), F32),
            jax.ShapeDtypeStruct((TS_DEV, LAT, LON), BF16),
        ],
        scratch_shapes=[pltpu.VMEM((2, LAT, 128), F32)],
        compiler_params=pltpu.CompilerParams(vmem_limit_bytes=20 * MIB),
        name="tile_sum",
    )(got)


def put_strips(strip, dtype):
    lane = lax.broadcasted_iota(jnp.int32, (LAT, 128), 1)

    def packed(planes, side):
        out = jnp.zeros((LAT, 128), F32)
        for k, plane in enumerate(planes):
            if side == 0:
                part = plane[:, :128]
                shift = HALO * k
            else:
                part = plane[:, LON - 128 :]
                shift = HALO * k + HALO
            moved = pltpu.roll(part, shift % 128, 1) if shift % 128 else part
            out = jnp.where((lane >= HALO * k) & (lane < HALO * k + HALO), moved, out)
        return out.astype(dtype)

    return packed(strip, 0), packed(strip, 1)


def pack_lon(arrays, dtype, name):
    counts = [a.shape[0] for a in arrays]

    def body(*refs):
        planes = [
            ref[k].astype(F32) for ref, count in zip(refs, counts) for k in range(count)
        ]
        refs[-2][...], refs[-1][...] = put_strips(planes, dtype)

    return pl.pallas_call(
        body,
        in_specs=vmem(*arrays),
        out_specs=vmem(0, 0),
        out_shape=[jax.ShapeDtypeStruct((LAT, 128), dtype)] * 2,
        name=name,
    )(*arrays)


def pack_lat(arrays, from_left, from_right, dtype, name):
    counts = [a.shape[0] for a in arrays]
    n = sum(counts)

    def body(*refs):
        up_ref, down_ref = refs[-2:]
        strips = jnp.concatenate(
            [refs[-4][...].astype(F32), refs[-3][...].astype(F32)], axis=1
        )
        planes = [
            ref[k].astype(F32) for ref, count in zip(refs, counts) for k in range(count)
        ] + [strips]
        up = jnp.concatenate([p[:HALO] for p in planes], axis=0)
        down = jnp.concatenate([p[LAT - HALO :] for p in planes], axis=0)
        up_ref[...] = up.astype(dtype)
        down_ref[...] = down.astype(dtype)

    return pl.pallas_call(
        body,
        in_specs=vmem(*arrays, 0, 0),
        out_specs=vmem(0, 0),
        out_shape=[jax.ShapeDtypeStruct(((n + 1) * HALO, LON), dtype)] * 2,
        name=name,
    )(*arrays, from_left, from_right)


def padded_plane(k, n, plane, left, right, up, down):
    lane = lax.broadcasted_iota(jnp.int32, (PAD_LAT, 128), 1)

    def rows(mid, top, low):
        zero = jnp.zeros((8 - HALO, mid.shape[1]), F32)
        return jnp.concatenate([zero, top, mid, low, zero], axis=0)

    def from_end(strips, side):
        return strips[n * HALO : (n + 1) * HALO, side * 128 : side * 128 + 128]

    main = rows(plane, up[k * HALO : (k + 1) * HALO], down[k * HALO : (k + 1) * HALO])
    lefts = rows(left, from_end(up, 0), from_end(down, 0))
    rights = rows(right, from_end(up, 1), from_end(down, 1))
    to_right = (-HALO * k) % 128
    to_left = (128 - HALO - HALO * k) % 128
    rights = pltpu.roll(rights, to_right, 1) if to_right else rights
    lefts = pltpu.roll(lefts, to_left, 1) if to_left else lefts
    side = jnp.where(lane < HALO, rights, jnp.where(lane >= 128 - HALO, lefts, 0.0))
    return jnp.concatenate([main, side], axis=1)


def pad_static(sigma, diffusivity, left, right, up, down):
    n = TRACERS + 1

    def body(s_ref, d_ref, l_ref, r_ref, u_ref, w_ref, out_ref):
        for k in range(n):
            plane = s_ref[k] if k < TRACERS else d_ref[0]
            out_ref[k] = padded_plane(
                k, n, plane, l_ref[...], r_ref[...], u_ref[...], w_ref[...]
            )

    return pl.pallas_call(
        body,
        in_specs=vmem(*range(6)),
        out_specs=pl.BlockSpec(memory_space=pltpu.VMEM),
        out_shape=jax.ShapeDtypeStruct((n, PAD_LAT, PAD_LON), F32),
        name="pad_static",
    )(sigma, diffusivity, left, right, up, down)


def diffuse(adj, before, after, left, right, up, down, static, taps):
    n = TS_DEV + 2 * HB

    def body(
        taps_ref, a_ref, b_ref, f_ref, l_ref, r_ref, u_ref, w_ref, st_ref, out_ref, pad_ref
    ):
        c = pl.program_id(0)

        @pl.when(c == 0)
        def _():
            left_, right_ = l_ref[...].astype(F32), r_ref[...].astype(F32)
            up_, down_ = u_ref[...].astype(F32), w_ref[...].astype(F32)
            for k in range(n):
                if k < HB:
                    plane = b_ref[k].astype(F32)
                elif k < HB + TS_DEV:
                    plane = a_ref[k - HB]
                else:
                    plane = f_ref[k - HB - TS_DEV].astype(F32)
                pad_ref[k] = padded_plane(k, n, plane, left_, right_, up_, down_)

        for t in range(TS_DEV):
            banded = taps_ref[c, 0] * pad_ref[t]
            for k in range(1, 2 * HB + 1):
                banded = banded + taps_ref[c, k] * pad_ref[t + k]
            field = st_ref[c] * banded
            for _ in range(KSTEPS):
                beside = (
                    pltpu.roll(field, 1, 1)
                    + pltpu.roll(field, PAD_LON - 1, 1)
                    + pltpu.roll(field, 1, 0)
                    + pltpu.roll(field, PAD_LAT - 1, 0)
                )
                field = field + st_ref[TRACERS] * (beside - 4.0 * field)
            out_ref[0, t] = st_ref[c, 8 : 8 + LAT, :LON] * field[8 : 8 + LAT, :LON]

    whole = [pl.BlockSpec(memory_space=pltpu.VMEM)] * 8
    return pl.pallas_call(
        body,
        grid=(TRACERS,),
        in_specs=[pl.BlockSpec(memory_space=pltpu.SMEM)] + whole,
        out_specs=pl.BlockSpec((1, TS_DEV, LAT, LON), lambda c: (c, 0, 0, 0)),
        out_shape=jax.ShapeDtypeStruct((TRACERS, TS_DEV, LAT, LON), F32),
        scratch_shapes=[pltpu.VMEM((n, PAD_LAT, PAD_LON), F32)],
        compiler_params=pltpu.CompilerParams(vmem_limit_bytes=20 * MIB),
        name="diffuse",
    )(taps, adj, before, after, left, right, up, down, static)


def steps(axis, periodic):
    count = lax.axis_size(axis)
    forward = [(i, i + 1) for i in range(count - 1)]
    if periodic:
        forward.append((count - 1, 0))
    return forward, [(b, a) for a, b in forward]


def halos(arrays, dtype, name):
    east, west = steps("gx", True)
    south, north = steps("gy", False)
    to_left, to_right = pack_lon(arrays, dtype, name + "_lon")
    left = lax.ppermute(to_right, "gx", east)
    right = lax.ppermute(to_left, "gx", west)
    to_up, to_down = pack_lat(arrays, left, right, dtype, name + "_lat")
    up = lax.ppermute(to_down, "gy", south)
    down = lax.ppermute(to_up, "gy", north)
    return left, right, up, down


def per_device(residual, footprint, tile_id, step_id, block_id, sigma, taps, diffusivity):
    bins = tile_id[:, 0] * BINS + step_id * 16 + (block_id % 2) * 8 + block_id // 2
    plane = diffusivity[None]
    static = pad_static(sigma, plane, *halos((sigma, plane), F32, "static"))
    partial_sums = bin_sums(
        bins[None, :], residual.astype(F32)[None, :], footprint, 4
    )
    got = lax.all_to_all(
        partial_sums.reshape(TILES, BINS, FP), ("gy", "gx"), 0, 0, tiled=True
    )
    adj, adj16 = tile_sum(got)
    later, sooner = steps("ta", False)
    before = lax.ppermute(adj16[TS_DEV - HB :], "ta", later)
    after = lax.ppermute(adj16[:HB], "ta", sooner)
    sides = halos((before, adj, after), BF16, "adjoint")
    return diffuse(adj, before, after, *sides, static, taps)


def solution(mesh):
    return jax.shard_map(
        per_device,
        mesh=mesh,
        in_specs=(
            P(("ta", "gy", "gx")),
            P(("ta", "gy", "gx"), None),
            P(("ta", "gy", "gx"), None),
            P(("ta", "gy", "gx")),
            P(("ta", "gy", "gx")),
            P(None, "gy", "gx"),
            P(),
            P("gy", "gx"),
        ),
        out_specs=P(None, "ta", "gy", "gx"),
        check_vma=False,
    )
```

```python
import jax
import jax.numpy as jnp
from jax import lax
from jax.experimental import pallas as pl
from jax.experimental.pallas import tpu as pltpu
from jax.sharding import PartitionSpec as P

TS_DEV = 4
TRACERS = 4
HB = 2
KSTEPS = 4
LAT = 64
LON = 256
FP = 1024
HALF = FP // 2
BINS = 64
SND = 2048
TILES = 32
PAD_LAT = LAT + 16
PAD_LON = LON + 128
HALO = KSTEPS
F32 = jnp.float32
BF16 = jnp.bfloat16
MIB = 1 << 20


def bin_sums(bins, residual, footprint, half, col_blocks):
    cols = HALF // col_blocks
    rows = 512

    def body(bins_ref, res_ref, fp_ref, out_ref, sel_ref):
        @pl.when(pl.program_id(0) == 0)
        def _():
            number = lax.broadcasted_iota(jnp.int32, (16, SND), 0)

            @pl.loop(0, TILES * BINS // 16, unroll=4)
            def _(m):
                first = m * 16
                hit = (bins_ref[...] - first) == number
                sel_ref[pl.ds(pl.multiple_of(first, 16), 16), :] = jnp.where(
                    hit, res_ref[...], 0.0
                ).astype(BF16)

        @pl.loop(0, TILES * BINS // rows)
        def _(m):
            at = pl.ds(pl.multiple_of(m * rows, rows), rows)
            out_ref[at, :] = jnp.dot(
                sel_ref[at, :], fp_ref[...], preferred_element_type=F32
            ).astype(BF16)

    return pl.pallas_call(
        body,
        grid=(col_blocks,),
        in_specs=[
            pl.BlockSpec((1, SND), lambda c: (0, 0)),
            pl.BlockSpec((1, SND), lambda c: (0, 0)),
            pl.BlockSpec((SND, cols), lambda c: (0, half * col_blocks + c)),
        ],
        out_specs=pl.BlockSpec((TILES * BINS, cols), lambda c: (0, c)),
        out_shape=jax.ShapeDtypeStruct((TILES * BINS, HALF), BF16),
        scratch_shapes=[pltpu.VMEM((TILES * BINS, SND), BF16)],
        compiler_params=pltpu.CompilerParams(vmem_limit_bytes=58 * MIB),
        cost_estimate=pl.CostEstimate(
            flops=2 * TILES * BINS * SND * HALF, bytes_accessed=4 * MIB, transcendentals=0
        ),
        name="bin_sums",
    )(bins, residual, footprint)


def sum_first(got, blocks):
    count, rows, cols = got.shape

    def body(got_ref, out_ref):
        total = got_ref[0].astype(F32)
        for s in range(1, count):
            total = total + got_ref[s].astype(F32)
        out_ref[...] = total.astype(BF16)

    return pl.pallas_call(
        body,
        grid=(blocks,),
        in_specs=[pl.BlockSpec((count, rows // blocks, cols), lambda t: (0, t, 0))],
        out_specs=pl.BlockSpec((rows // blocks, cols), lambda t: (t, 0)),
        out_shape=jax.ShapeDtypeStruct((rows, cols), BF16),
        compiler_params=pltpu.CompilerParams(vmem_limit_bytes=8 * MIB),
        name="sum_first",
    )(got)


def tile_sum(summed, got):
    count = got.shape[0]
    half_i = HALF // 128

    def body(sum_ref, got_ref, adj_ref, send_ref, half_ref):
        low = sum_ref[...].astype(F32)
        high = got_ref[0].astype(F32)
        for s in range(1, count):
            high = high + got_ref[s].astype(F32)
        for bc in range(2):
            for i in range(8):
                part, k = (low, i) if i < half_i else (high, i - half_i)
                half_ref[bc, pl.ds(i, 8, stride=8), :] = part[
                    bc * 8 : bc * 8 + 8, k * 128 : k * 128 + 128
                ]
            adj_ref[0, :, bc * 128 : bc * 128 + 128] = half_ref[bc]
        send_ref[...] = adj_ref[...].astype(BF16)

    return pl.pallas_call(
        body,
        grid=(TS_DEV,),
        in_specs=[
            pl.BlockSpec((BINS // TS_DEV, HALF), lambda t: (t, 0)),
            pl.BlockSpec((count, BINS // TS_DEV, HALF), lambda t: (0, t, 0)),
        ],
        out_specs=[pl.BlockSpec((1, LAT, LON), lambda t: (t, 0, 0))] * 2,
        out_shape=[
            jax.ShapeDtypeStruct((TS_DEV, LAT, LON), F32),
            jax.ShapeDtypeStruct((TS_DEV, LAT, LON), BF16),
        ],
        scratch_shapes=[pltpu.VMEM((2, LAT, 128), F32)],
        compiler_params=pltpu.CompilerParams(vmem_limit_bytes=8 * MIB),
        name="tile_sum",
    )(summed, got)


def put_strips(strip, dtype):
    lane = lax.broadcasted_iota(jnp.int32, (LAT, 128), 1)

    def packed(planes, side):
        out = jnp.zeros((LAT, 128), F32)
        for k, plane in enumerate(planes):
            if side == 0:
                part = plane[:, :128]
                shift = HALO * k
            else:
                part = plane[:, LON - 128 :]
                shift = HALO * k + HALO
            moved = pltpu.roll(part, shift % 128, 1) if shift % 128 else part
            out = jnp.where((lane >= HALO * k) & (lane < HALO * k + HALO), moved, out)
        return out.astype(dtype)

    return packed(strip, 0), packed(strip, 1)


def pack_lon(arrays, dtype, name):
    counts = [a.shape[0] for a in arrays]

    def body(*refs):
        planes = [
            ref[k].astype(F32) for ref, count in zip(refs, counts) for k in range(count)
        ]
        refs[-2][...], refs[-1][...] = put_strips(planes, dtype)

    return pl.pallas_call(
        body,
        out_shape=[jax.ShapeDtypeStruct((LAT, 128), dtype)] * 2,
        compiler_params=pltpu.CompilerParams(vmem_limit_bytes=8 * MIB),
        name=name,
    )(*arrays)


def pack_lat(arrays, from_left, from_right, dtype, name):
    counts = [a.shape[0] for a in arrays]
    n = sum(counts)

    def body(*refs):
        up_ref, down_ref = refs[-2:]
        strips = jnp.concatenate(
            [refs[-4][...].astype(F32), refs[-3][...].astype(F32)], axis=1
        )
        planes = [
            ref[k].astype(F32) for ref, count in zip(refs, counts) for k in range(count)
        ] + [strips]
        up = jnp.concatenate([p[:HALO] for p in planes], axis=0)
        down = jnp.concatenate([p[LAT - HALO :] for p in planes], axis=0)
        up_ref[...] = up.astype(dtype)
        down_ref[...] = down.astype(dtype)

    return pl.pallas_call(
        body,
        out_shape=[jax.ShapeDtypeStruct(((n + 1) * HALO, LON), dtype)] * 2,
        compiler_params=pltpu.CompilerParams(vmem_limit_bytes=8 * MIB),
        name=name,
    )(*arrays, from_left, from_right)


def padded_plane(k, n, plane, left, right, up, down):
    lane = lax.broadcasted_iota(jnp.int32, (PAD_LAT, 128), 1)

    def rows(mid, top, low):
        zero = jnp.zeros((8 - HALO, mid.shape[1]), F32)
        return jnp.concatenate([zero, top, mid, low, zero], axis=0)

    def from_end(strips, side):
        return strips[n * HALO : (n + 1) * HALO, side * 128 : side * 128 + 128]

    main = rows(plane, up[k * HALO : (k + 1) * HALO], down[k * HALO : (k + 1) * HALO])
    lefts = rows(left, from_end(up, 0), from_end(down, 0))
    rights = rows(right, from_end(up, 1), from_end(down, 1))
    to_right = (-HALO * k) % 128
    to_left = (128 - HALO - HALO * k) % 128
    rights = pltpu.roll(rights, to_right, 1) if to_right else rights
    lefts = pltpu.roll(lefts, to_left, 1) if to_left else lefts
    side = jnp.where(lane < HALO, rights, jnp.where(lane >= 128 - HALO, lefts, 0.0))
    return jnp.concatenate([main, side], axis=1)


def diffuse(adj, before, after, sigma, diffusivity, left, right, up, down, taps):
    n = TS_DEV + 2 * HB
    count = n + TRACERS + 1

    def body(
        taps_ref, a_ref, b_ref, f_ref, s_ref, d_ref, l_ref, r_ref, u_ref, w_ref, out_ref, pad_ref
    ):
        c = pl.program_id(0)

        @pl.when(c == 0)
        def _():
            planes = [b_ref[k].astype(F32) for k in range(HB)]
            planes += [a_ref[k] for k in range(TS_DEV)]
            planes += [f_ref[k].astype(F32) for k in range(HB)]
            planes += [s_ref[k] for k in range(TRACERS)] + [d_ref[0]]
            for k in range(count):
                pad_ref[k] = padded_plane(
                    k, count, planes[k], l_ref[...], r_ref[...], u_ref[...], w_ref[...]
                )

        for t in range(TS_DEV):
            banded = taps_ref[c, 0] * pad_ref[t]
            for k in range(1, 2 * HB + 1):
                banded = banded + taps_ref[c, k] * pad_ref[t + k]
            field = pad_ref[n + c] * banded
            for _ in range(KSTEPS):
                beside = (
                    pltpu.roll(field, 1, 1)
                    + pltpu.roll(field, PAD_LON - 1, 1)
                    + pltpu.roll(field, 1, 0)
                    + pltpu.roll(field, PAD_LAT - 1, 0)
                )
                field = field + pad_ref[count - 1] * (beside - 4.0 * field)
            out_ref[0, t] = s_ref[c] * field[8 : 8 + LAT, :LON]

    def whole(a):
        return pl.BlockSpec(a.shape, lambda c: (0,) * a.ndim)

    arrays = (adj, before, after, sigma, diffusivity, left, right, up, down)
    return pl.pallas_call(
        body,
        grid=(TRACERS,),
        in_specs=[pl.BlockSpec(memory_space=pltpu.SMEM)] + [whole(a) for a in arrays],
        out_specs=pl.BlockSpec((1, TS_DEV, LAT, LON), lambda c: (c, 0, 0, 0)),
        out_shape=jax.ShapeDtypeStruct((TRACERS, TS_DEV, LAT, LON), F32),
        scratch_shapes=[pltpu.VMEM((count, PAD_LAT, PAD_LON), F32)],
        compiler_params=pltpu.CompilerParams(vmem_limit_bytes=24 * MIB),
        name="diffuse",
    )(taps, *arrays)


def steps(axis, periodic):
    count = lax.axis_size(axis)
    forward = [(i, i + 1) for i in range(count - 1)]
    if periodic:
        forward.append((count - 1, 0))
    return forward, [(b, a) for a, b in forward]


def halos(arrays, dtype, name):
    east, west = steps("gx", True)
    south, north = steps("gy", False)
    to_left, to_right = pack_lon(arrays, dtype, name + "_lon")
    left = lax.ppermute(to_right, "gx", east)
    right = lax.ppermute(to_left, "gx", west)
    to_up, to_down = pack_lat(arrays, left, right, dtype, name + "_lat")
    up = lax.ppermute(to_down, "gy", south)
    down = lax.ppermute(to_up, "gy", north)
    return left, right, up, down


def per_device(residual, footprint, tile_id, step_id, block_id, sigma, taps, diffusivity):
    rows_gy, cols_gx = lax.axis_size("gy"), lax.axis_size("gx")
    local = step_id * 16 + (block_id % 2) * 8 + block_id // 2
    tile = tile_id[:, 0]
    gy_first = tile * BINS + local
    gx_first = ((tile % cols_gx) * rows_gy + tile // cols_gx) * BINS + local
    weight = residual.astype(F32)[None, :]
    by_gy = bin_sums(gy_first[None, :], weight, footprint, 1, 2)
    by_gx = bin_sums(gx_first[None, :], weight, footprint, 0, 2)
    some_gy = lax.psum_scatter(by_gy, "gy", scatter_dimension=0, tiled=True)
    got_gx = lax.all_to_all(
        by_gx.reshape(cols_gx, rows_gy * BINS, HALF), "gx", 0, 0, tiled=True
    )
    some_gx = sum_first(got_gx, rows_gy)
    all_gx = lax.psum_scatter(some_gx, "gy", scatter_dimension=0, tiled=True)
    got_gy = lax.all_to_all(
        some_gy.reshape(cols_gx, BINS, HALF), "gx", 0, 0, tiled=True
    )
    adj, adj16 = tile_sum(all_gx, got_gy)
    later, sooner = steps("ta", False)
    before = lax.ppermute(adj16[TS_DEV - HB :], "ta", later)
    after = lax.ppermute(adj16[:HB], "ta", sooner)
    plane = diffusivity[None]
    sides = halos((before, adj, after, sigma, plane), F32, "halo")
    return diffuse(adj, before, after, sigma, plane, *sides, taps)


def solution(mesh):
    return jax.shard_map(
        per_device,
        mesh=mesh,
        in_specs=(
            P(("ta", "gy", "gx")),
            P(("ta", "gy", "gx"), None),
            P(("ta", "gy", "gx"), None),
            P(("ta", "gy", "gx")),
            P(("ta", "gy", "gx")),
            P(None, "gy", "gx"),
            P(),
            P("gy", "gx"),
        ),
        out_specs=P(None, "ta", "gy", "gx"),
        check_vma=False,
    )
```

```python
import jax
import jax.numpy as jnp
from jax import lax
from jax.experimental import pallas as pl
from jax.experimental.pallas import tpu as pltpu
from jax.sharding import PartitionSpec as P

TS_DEV = 4
TRACERS = 4
HB = 2
KSTEPS = 4
LAT = 64
LON = 256
FP = 1024
HALF = FP // 2
BINS = 64
SND = 2048
N_GY = 4
N_GX = 8
TILES = N_GY * N_GX
PAD_LAT = LAT + 16
PAD_LON = LON + 128
HALO = KSTEPS
F32 = jnp.float32
BF16 = jnp.bfloat16
MIB = 1 << 20


def bin_sums(ids, residual, footprint, first_col, cols, blocks, gx_first):
    width = cols // blocks
    parts = 1 if gx_first else N_GY
    rows = TILES * BINS // parts

    def body(tile_ref, step_ref, block_ref, res_ref, fp_ref, *refs):
        sel_ref = refs[-1]

        @pl.when(pl.program_id(0) == 0)
        def _():
            tile = tile_ref[...].reshape(1, SND)
            block = block_ref[...].reshape(1, SND)
            local = step_ref[...].reshape(1, SND) * 16 + (block & 1) * 8 + (block >> 1)
            away = (tile // N_GX - lax.axis_index("gy")) & (N_GY - 1)
            column = tile & (N_GX - 1)
            order = column * N_GY + away if gx_first else away * N_GX + column
            bins = (order * BINS + local).astype(jnp.int16)
            weight = jnp.broadcast_to(res_ref[...].reshape(1, SND).astype(BF16), (16, SND))
            number = lax.broadcasted_iota(jnp.int32, (16, SND), 0).astype(jnp.int16)

            @pl.loop(0, TILES * BINS // 16, unroll=4)
            def _(m):
                hit = (bins - (m * 16).astype(jnp.int16)) == number
                sel_ref[pl.ds(pl.multiple_of(m * 16, 16), 16), :] = jnp.where(
                    hit, weight, jnp.zeros((16, SND), BF16)
                )

        for k, out_ref in enumerate(refs[:-1]):
            chunk = min(rows, 1024)
            for m in range(rows // chunk):
                out_ref[m * chunk : m * chunk + chunk, :] = jnp.dot(
                    sel_ref[k * rows + m * chunk : k * rows + m * chunk + chunk, :],
                    fp_ref[...],
                    preferred_element_type=F32,
                ).astype(BF16)

    one = pl.BlockSpec((SND,), lambda c: (0,))
    return pl.pallas_call(
        body,
        grid=(blocks,),
        in_specs=[one] * 4 + [pl.BlockSpec((SND, width), lambda c: (0, first_col // width + c))],
        out_specs=[pl.BlockSpec((rows, width), lambda c: (0, c))] * parts,
        out_shape=[jax.ShapeDtypeStruct((rows, cols), BF16)] * parts,
        scratch_shapes=[pltpu.VMEM((TILES * BINS, SND), BF16)],
        compiler_params=pltpu.CompilerParams(vmem_limit_bytes=58 * MIB),
        cost_estimate=pl.CostEstimate(
            flops=4 * TILES * BINS * SND * cols, bytes_accessed=8 * SND * cols, transcendentals=0
        ),
        name="bin_sums",
    )(*ids, residual, footprint)


def sum_first(got, parts):
    count, rows, cols = got.shape
    each = rows // parts

    def body(got_ref, *out_refs):
        for k, out_ref in enumerate(out_refs):
            at = pl.ds(k * each, each)
            total = got_ref[0, at].astype(F32)
            for s in range(1, count):
                total = total + got_ref[s, at].astype(F32)
            out_ref[...] = total.astype(BF16)

    return pl.pallas_call(
        body,
        out_shape=[jax.ShapeDtypeStruct((each, cols), BF16)] * parts,
        compiler_params=pltpu.CompilerParams(vmem_limit_bytes=12 * MIB),
        name="sum_first",
    )(got)


def sum_arrays(arrays):
    rows, cols = arrays[0].shape
    step = 128

    def body(*refs):
        total = refs[0][...].astype(F32)
        for ref in refs[1:-1]:
            total = total + ref[...].astype(F32)
        refs[-1][...] = total.astype(BF16)

    return pl.pallas_call(
        body,
        grid=(rows // step,),
        in_specs=[pl.BlockSpec((step, cols), lambda t: (t, 0))] * len(arrays),
        out_specs=pl.BlockSpec((step, cols), lambda t: (t, 0)),
        out_shape=jax.ShapeDtypeStruct((rows, cols), BF16),
        compiler_params=pltpu.CompilerParams(vmem_limit_bytes=8 * MIB),
        name="sum_arrays",
    )(*arrays)


def tile_sum(summed, got):
    count = got.shape[0]
    half_i = HALF // 128

    def body(*refs):
        got_ref, adj_ref, low_ref, high_ref, half_ref = refs[-5:]
        low = refs[0][...].astype(F32)
        for ref in refs[1:-5]:
            low = low + ref[...].astype(F32)
        high = got_ref[0].astype(F32)
        for s in range(1, count):
            high = high + got_ref[s].astype(F32)
        for t in range(TS_DEV):
            for bc in range(2):
                row = t * 16 + bc * 8
                for i in range(8):
                    part, k = (low, i) if i < half_i else (high, i - half_i)
                    half_ref[t, bc, pl.ds(i, 8, stride=8), :] = part[
                        row : row + 8, k * 128 : k * 128 + 128
                    ]
                adj_ref[t, :, bc * 128 : bc * 128 + 128] = half_ref[t, bc]
        low_ref[...] = adj_ref[:HB].astype(BF16)
        high_ref[...] = adj_ref[TS_DEV - HB :].astype(BF16)

    return pl.pallas_call(
        body,
        out_shape=[
            jax.ShapeDtypeStruct((TS_DEV, LAT, LON), F32),
            jax.ShapeDtypeStruct((HB, LAT, LON), BF16),
            jax.ShapeDtypeStruct((HB, LAT, LON), BF16),
        ],
        scratch_shapes=[pltpu.VMEM((TS_DEV, 2, LAT, 128), F32)],
        compiler_params=pltpu.CompilerParams(vmem_limit_bytes=8 * MIB),
        name="tile_sum",
    )(*summed, got)


def put_strips(strip, dtype):
    lane = lax.broadcasted_iota(jnp.int32, (LAT, 128), 1)

    def packed(planes, side):
        out = jnp.zeros((LAT, 128), F32)
        for k, plane in enumerate(planes):
            if side == 0:
                part = plane[:, :128]
                shift = HALO * k
            else:
                part = plane[:, LON - 128 :]
                shift = HALO * k + HALO
            moved = pltpu.roll(part, shift % 128, 1) if shift % 128 else part
            out = jnp.where((lane >= HALO * k) & (lane < HALO * k + HALO), moved, out)
        return out.astype(dtype)

    return packed(strip, 0), packed(strip, 1)


def pack_lon(arrays, dtype, name):
    counts = [a.shape[0] for a in arrays]

    def body(*refs):
        planes = [
            ref[k].astype(F32) for ref, count in zip(refs, counts) for k in range(count)
        ]
        refs[-2][...], refs[-1][...] = put_strips(planes, dtype)

    return pl.pallas_call(
        body,
        out_shape=[jax.ShapeDtypeStruct((LAT, 128), dtype)] * 2,
        compiler_params=pltpu.CompilerParams(vmem_limit_bytes=8 * MIB),
        name=name,
    )(*arrays)


def pack_lat(arrays, from_left, from_right, dtype, name):
    counts = [a.shape[0] for a in arrays]
    n = sum(counts)

    def body(*refs):
        up_ref, down_ref = refs[-2:]
        strips = jnp.concatenate(
            [refs[-4][...].astype(F32), refs[-3][...].astype(F32)], axis=1
        )
        planes = [
            ref[k].astype(F32) for ref, count in zip(refs, counts) for k in range(count)
        ] + [strips]
        up = jnp.concatenate([p[:HALO] for p in planes], axis=0)
        down = jnp.concatenate([p[LAT - HALO :] for p in planes], axis=0)
        up_ref[...] = up.astype(dtype)
        down_ref[...] = down.astype(dtype)

    return pl.pallas_call(
        body,
        out_shape=[jax.ShapeDtypeStruct(((n + 1) * HALO, LON), dtype)] * 2,
        compiler_params=pltpu.CompilerParams(vmem_limit_bytes=8 * MIB),
        name=name,
    )(*arrays, from_left, from_right)


def padded_plane(k, n, plane, left, right, up, down):
    lane = lax.broadcasted_iota(jnp.int32, (PAD_LAT, 128), 1)

    def rows(mid, top, low):
        zero = jnp.zeros((8 - HALO, mid.shape[1]), F32)
        return jnp.concatenate([zero, top, mid, low, zero], axis=0)

    def from_end(strips, side):
        return strips[n * HALO : (n + 1) * HALO, side * 128 : side * 128 + 128]

    main = rows(plane, up[k * HALO : (k + 1) * HALO], down[k * HALO : (k + 1) * HALO])
    lefts = rows(left, from_end(up, 0), from_end(down, 0))
    rights = rows(right, from_end(up, 1), from_end(down, 1))
    to_right = (-HALO * k) % 128
    to_left = (128 - HALO - HALO * k) % 128
    rights = pltpu.roll(rights, to_right, 1) if to_right else rights
    lefts = pltpu.roll(lefts, to_left, 1) if to_left else lefts
    side = jnp.where(lane < HALO, rights, jnp.where(lane >= 128 - HALO, lefts, 0.0))
    return jnp.concatenate([main, side], axis=1)


def diffuse(adj, before, after, sigma, diffusivity, left, right, up, down, taps):
    n = TS_DEV + 2 * HB
    count = n + TRACERS + 1

    def body(
        taps_ref, a_ref, b_ref, f_ref, s_ref, d_ref, l_ref, r_ref, u_ref, w_ref, out_ref, pad_ref
    ):
        c = pl.program_id(0)

        @pl.when(c == 0)
        def _():
            planes = [b_ref[k].astype(F32) for k in range(HB)]
            planes += [a_ref[k] for k in range(TS_DEV)]
            planes += [f_ref[k].astype(F32) for k in range(HB)]
            planes += [s_ref[k] for k in range(TRACERS)] + [d_ref[0]]
            for k in range(count):
                pad_ref[k] = padded_plane(
                    k, count, planes[k], l_ref[...], r_ref[...], u_ref[...], w_ref[...]
                )

        for t in range(TS_DEV):
            banded = taps_ref[c, 0] * pad_ref[t]
            for k in range(1, 2 * HB + 1):
                banded = banded + taps_ref[c, k] * pad_ref[t + k]
            field = pad_ref[n + c] * banded
            for _ in range(KSTEPS):
                beside = (
                    pltpu.roll(field, 1, 1)
                    + pltpu.roll(field, PAD_LON - 1, 1)
                    + pltpu.roll(field, 1, 0)
                    + pltpu.roll(field, PAD_LAT - 1, 0)
                )
                field = field + pad_ref[count - 1] * (beside - 4.0 * field)
            out_ref[0, t] = s_ref[c] * field[8 : 8 + LAT, :LON]

    def whole(a):
        return pl.BlockSpec(a.shape, lambda c: (0,) * a.ndim)

    arrays = (adj, before, after, sigma, diffusivity, left, right, up, down)
    return pl.pallas_call(
        body,
        grid=(TRACERS,),
        in_specs=[pl.BlockSpec(memory_space=pltpu.SMEM)] + [whole(a) for a in arrays],
        out_specs=pl.BlockSpec((1, TS_DEV, LAT, LON), lambda c: (c, 0, 0, 0)),
        out_shape=jax.ShapeDtypeStruct((TRACERS, TS_DEV, LAT, LON), F32),
        scratch_shapes=[pltpu.VMEM((count, PAD_LAT, PAD_LON), F32)],
        compiler_params=pltpu.CompilerParams(vmem_limit_bytes=24 * MIB),
        name="diffuse",
    )(taps, *arrays)


def steps(axis, periodic):
    count = lax.axis_size(axis)
    forward = [(i, i + 1) for i in range(count - 1)]
    if periodic:
        forward.append((count - 1, 0))
    return forward, [(b, a) for a, b in forward]


def halos(arrays, dtype, name):
    east, west = steps("gx", True)
    south, north = steps("gy", False)
    to_left, to_right = pack_lon(arrays, dtype, name + "_lon")
    left = lax.ppermute(to_right, "gx", east)
    right = lax.ppermute(to_left, "gx", west)
    to_up, to_down = pack_lat(arrays, left, right, dtype, name + "_lat")
    up = lax.ppermute(to_down, "gy", south)
    down = lax.ppermute(to_up, "gy", north)
    return left, right, up, down


def along_gy(parts):
    return [parts[0]] + [
        lax.ppermute(parts[k], "gy", [(i, (i + k) % N_GY) for i in range(N_GY)])
        for k in range(1, N_GY)
    ]


def along_gx(rows):
    return lax.all_to_all(
        rows.reshape(N_GX, rows.shape[0] // N_GX, HALF), "gx", 0, 0, tiled=True
    )


def per_device(residual, footprint, tile_id, step_id, block_id, sigma, taps, diffusivity):
    ids = (tile_id[:, 0], step_id, block_id)
    weight = residual.astype(F32)
    [first_gx] = bin_sums(ids, weight, footprint, 0, HALF, 2, True)
    got_gx = along_gx(first_gx)
    weight, first_gx = lax.optimization_barrier((weight, first_gx))
    first_gy = bin_sums(ids, weight, footprint, HALF, HALF, 2, False)
    some_gy = sum_arrays(along_gy(first_gy))
    all_gx = along_gy(sum_first(got_gx, N_GY))
    all_gy = along_gx(some_gy)
    adj, low, high = tile_sum(all_gx, all_gy)
    later, sooner = steps("ta", False)
    before = lax.ppermute(high, "ta", later)
    after = lax.ppermute(low, "ta", sooner)
    plane = diffusivity[None]
    sides = halos((before, adj, after, sigma, plane), F32, "halo")
    return diffuse(adj, before, after, sigma, plane, *sides, taps)


def solution(mesh):
    return jax.shard_map(
        per_device,
        mesh=mesh,
        in_specs=(
            P(("ta", "gy", "gx")),
            P(("ta", "gy", "gx"), None),
            P(("ta", "gy", "gx"), None),
            P(("ta", "gy", "gx")),
            P(("ta", "gy", "gx")),
            P(None, "gy", "gx"),
            P(),
            P("gy", "gx"),
        ),
        out_specs=P(None, "ta", "gy", "gx"),
        check_vma=False,
    )
```

```python
import jax
import jax.numpy as jnp
from jax import lax
from jax.experimental import pallas as pl
from jax.experimental.pallas import tpu as pltpu
from jax.sharding import PartitionSpec as P

TS_DEV = 4
TRACERS = 4
HB = 2
KSTEPS = 4
LAT = 64
LON = 256
FP = 1024
HALF = FP // 2
BINS = 64
SND = 2048
N_GY = 4
N_GX = 8
TILES = N_GY * N_GX
PAD_LON = LON + 128
HALO = KSTEPS
F32 = jnp.float32
BF16 = jnp.bfloat16
MIB = 1 << 20


def bin_sums(ids, residual, footprint):
    blocks = 4
    width = FP // blocks
    half = blocks // 2
    rows = N_GX * BINS

    def body(tile_ref, step_ref, block_ref, res_ref, fp_ref, first_ref, *refs):
        sel_ref = refs[-1]
        c = pl.program_id(0)

        @pl.when(c == 0)
        def _():
            tile = tile_ref[...].reshape(1, SND)
            block = block_ref[...].reshape(1, SND)
            local = step_ref[...].reshape(1, SND) * 16 + (block & 1) * 8 + (block >> 1)
            away = (tile // N_GX - lax.axis_index("gy")) & (N_GY - 1)
            bins = ((away * N_GX + (tile & (N_GX - 1))) * BINS + local).astype(jnp.int16)
            weight = jnp.broadcast_to(res_ref[...].reshape(1, SND).astype(BF16), (16, SND))
            number = lax.broadcasted_iota(jnp.int32, (16, SND), 0).astype(jnp.int16)

            @pl.loop(0, TILES * BINS // 16, unroll=4)
            def _(m):
                hit = (bins - (m * 16).astype(jnp.int16)) == number
                sel_ref[pl.ds(pl.multiple_of(m * 16, 16), 16), :] = jnp.where(
                    hit, weight, jnp.zeros((16, SND), BF16)
                )

        def sums(k):
            return jnp.dot(
                sel_ref[k * rows : (k + 1) * rows, :],
                fp_ref[...],
                preferred_element_type=F32,
            ).astype(BF16)

        @pl.when(c < half)
        def _():
            for k in range(N_GY):
                out = sums(k)
                for q in range(N_GX):
                    at = (q * N_GY + k) * BINS
                    first_ref[at : at + BINS, :] = out[q * BINS : (q + 1) * BINS]

        @pl.when(c >= half)
        def _():
            for k, out_ref in enumerate(refs[:-1]):
                out_ref[...] = sums(k)

    one = pl.BlockSpec((SND,), lambda c: (0,))
    outs = pl.pallas_call(
        body,
        grid=(blocks,),
        in_specs=[one] * 4 + [pl.BlockSpec((SND, width), lambda c: (0, c))],
        out_specs=[
            pl.BlockSpec((TILES * BINS, width), lambda c: (0, jnp.minimum(c, half - 1)))
        ]
        + [pl.BlockSpec((rows, width), lambda c: (0, jnp.maximum(c - half, 0)))] * N_GY,
        out_shape=[jax.ShapeDtypeStruct((TILES * BINS, HALF), BF16)]
        + [jax.ShapeDtypeStruct((rows, HALF), BF16)] * N_GY,
        scratch_shapes=[pltpu.VMEM((TILES * BINS, SND), BF16)],
        compiler_params=pltpu.CompilerParams(vmem_limit_bytes=58 * MIB),
        cost_estimate=pl.CostEstimate(
            flops=2 * TILES * BINS * SND * FP, bytes_accessed=8 * MIB, transcendentals=0
        ),
        name="bin_sums",
    )(*ids, residual, footprint)
    return outs[0], outs[1:]


def sum_first(got, parts):
    count, rows, cols = got.shape
    each = rows // parts

    def body(got_ref, *out_refs):
        for k, out_ref in enumerate(out_refs):
            at = pl.ds(k * each, each)
            total = got_ref[0, at].astype(F32)
            for s in range(1, count):
                total = total + got_ref[s, at].astype(F32)
            out_ref[...] = total.astype(BF16)

    return pl.pallas_call(
        body,
        out_shape=[jax.ShapeDtypeStruct((each, cols), BF16)] * parts,
        compiler_params=pltpu.CompilerParams(vmem_limit_bytes=12 * MIB),
        name="sum_first",
    )(got)


def sum_arrays(arrays):
    rows, cols = arrays[0].shape
    step = 128

    def body(*refs):
        total = refs[0][...].astype(F32)
        for ref in refs[1:-1]:
            total = total + ref[...].astype(F32)
        refs[-1][...] = total.astype(BF16)

    return pl.pallas_call(
        body,
        grid=(rows // step,),
        in_specs=[pl.BlockSpec((step, cols), lambda t: (t, 0))] * len(arrays),
        out_specs=pl.BlockSpec((step, cols), lambda t: (t, 0)),
        out_shape=jax.ShapeDtypeStruct((rows, cols), BF16),
        compiler_params=pltpu.CompilerParams(vmem_limit_bytes=8 * MIB),
        name="sum_arrays",
    )(*arrays)


def tile_sum(summed, got):
    count = got.shape[0]
    half_i = HALF // 128

    def body(*refs):
        got_ref, adj_ref, low_ref, high_ref, half_ref = refs[-5:]
        low = refs[0][...].astype(F32)
        for ref in refs[1:-5]:
            low = low + ref[...].astype(F32)
        high = got_ref[0].astype(F32)
        for s in range(1, count):
            high = high + got_ref[s].astype(F32)
        for t in range(TS_DEV):
            for bc in range(2):
                row = t * 16 + bc * 8
                for i in range(8):
                    part, k = (low, i) if i < half_i else (high, i - half_i)
                    half_ref[t, bc, pl.ds(i, 8, stride=8), :] = part[
                        row : row + 8, k * 128 : k * 128 + 128
                    ]
                adj_ref[t, :, bc * 128 : bc * 128 + 128] = half_ref[t, bc]
        low_ref[...] = adj_ref[:HB].astype(BF16)
        high_ref[...] = adj_ref[TS_DEV - HB :].astype(BF16)

    return pl.pallas_call(
        body,
        out_shape=[
            jax.ShapeDtypeStruct((TS_DEV, LAT, LON), F32),
            jax.ShapeDtypeStruct((HB, LAT, LON), BF16),
            jax.ShapeDtypeStruct((HB, LAT, LON), BF16),
        ],
        scratch_shapes=[pltpu.VMEM((TS_DEV, 2, LAT, 128), F32)],
        compiler_params=pltpu.CompilerParams(vmem_limit_bytes=8 * MIB),
        name="tile_sum",
    )(*summed, got)


def put_strips(strip, dtype):
    lane = lax.broadcasted_iota(jnp.int32, (LAT, 128), 1)

    def packed(planes, side):
        out = jnp.zeros((LAT, 128), F32)
        for k, plane in enumerate(planes):
            if side == 0:
                part = plane[:, :128]
                shift = HALO * k
            else:
                part = plane[:, LON - 128 :]
                shift = HALO * k + HALO
            moved = pltpu.roll(part, shift % 128, 1) if shift % 128 else part
            out = jnp.where((lane >= HALO * k) & (lane < HALO * k + HALO), moved, out)
        return out.astype(dtype)

    return packed(strip, 0), packed(strip, 1)


def pack_lon(arrays, dtype, name):
    counts = [a.shape[0] for a in arrays]

    def body(*refs):
        planes = [
            ref[k].astype(F32) for ref, count in zip(refs, counts) for k in range(count)
        ]
        refs[-2][...], refs[-1][...] = put_strips(planes, dtype)

    return pl.pallas_call(
        body,
        out_shape=[jax.ShapeDtypeStruct((LAT, 128), dtype)] * 2,
        compiler_params=pltpu.CompilerParams(vmem_limit_bytes=8 * MIB),
        name=name,
    )(*arrays)


def pack_lat(arrays, from_left, from_right, dtype, name):
    counts = [a.shape[0] for a in arrays]
    n = sum(counts)

    def body(*refs):
        up_ref, down_ref = refs[-2:]
        strips = jnp.concatenate(
            [refs[-4][...].astype(F32), refs[-3][...].astype(F32)], axis=1
        )
        planes = [
            ref[k].astype(F32) for ref, count in zip(refs, counts) for k in range(count)
        ] + [strips]
        up = jnp.concatenate([p[:HALO] for p in planes], axis=0)
        down = jnp.concatenate([p[LAT - HALO :] for p in planes], axis=0)
        up_ref[...] = up.astype(dtype)
        down_ref[...] = down.astype(dtype)

    return pl.pallas_call(
        body,
        out_shape=[jax.ShapeDtypeStruct(((n + 1) * HALO, LON), dtype)] * 2,
        compiler_params=pltpu.CompilerParams(vmem_limit_bytes=8 * MIB),
        name=name,
    )(*arrays, from_left, from_right)


def beside_lon(k, plane, left, right):
    lane = lax.broadcasted_iota(jnp.int32, right.shape, 1)
    to_right = (-HALO * k) % 128
    to_left = (128 - HALO - HALO * k) % 128
    right = pltpu.roll(right, to_right, 1) if to_right else right
    left = pltpu.roll(left, to_left, 1) if to_left else left
    side = jnp.where(lane < HALO, right, jnp.where(lane >= 128 - HALO, left, 0.0))
    return jnp.concatenate([plane, side], axis=1)


def covariance(c, taps_ref, pad_ref, rows):
    n = TS_DEV + 2 * HB
    banded = taps_ref[c, 0] * pad_ref[0:TS_DEV]
    for k in range(1, 2 * HB + 1):
        banded = banded + taps_ref[c, k] * pad_ref[k : k + TS_DEV]
    field = pad_ref[n + c][None] * banded
    for _ in range(KSTEPS):
        beside = (
            pltpu.roll(field, 1, 2)
            + pltpu.roll(field, PAD_LON - 1, 2)
            + pltpu.roll(field, 1, 1)
            + pltpu.roll(field, rows - 1, 1)
        )
        field = field + pad_ref[n + TRACERS][None] * (beside - 4.0 * field)
    return field


def planes_of(refs):
    return [ref[k].astype(F32) for ref in refs for k in range(ref.shape[0])]


def diffuse_inner(arrays, left, right, taps):
    count = TS_DEV + 2 * HB + TRACERS + 1

    def body(taps_ref, *refs):
        l_ref, r_ref, out_ref, pad_ref = refs[-4:]
        c = pl.program_id(0)

        @pl.when(c == 0)
        def _():
            for k, plane in enumerate(planes_of(refs[:-4])):
                pad_ref[k] = beside_lon(k, plane, l_ref[...], r_ref[...])

        field = covariance(c, taps_ref, pad_ref, LAT)
        scale = pad_ref[TS_DEV + 2 * HB + c, :, :LON]
        out_ref[0] = scale[None] * field[:, :, :LON]

    def whole(a):
        return pl.BlockSpec(a.shape, lambda c: (0,) * a.ndim)

    operands = (*arrays, left, right)
    return pl.pallas_call(
        body,
        grid=(TRACERS,),
        in_specs=[pl.BlockSpec(memory_space=pltpu.SMEM)] + [whole(a) for a in operands],
        out_specs=pl.BlockSpec((1, TS_DEV, LAT, LON), lambda c: (c, 0, 0, 0)),
        out_shape=jax.ShapeDtypeStruct((TRACERS, TS_DEV, LAT, LON), F32),
        scratch_shapes=[pltpu.VMEM((count, LAT, PAD_LON), F32)],
        compiler_params=pltpu.CompilerParams(vmem_limit_bytes=20 * MIB),
        cost_estimate=pl.CostEstimate(
            flops=200 * MIB, bytes_accessed=16 * MIB, transcendentals=0
        ),
        name="diffuse_inner",
    )(taps, *operands)


def diffuse_edges(inner, arrays, left, right, up, down, taps):
    n = TS_DEV + 2 * HB
    count = n + TRACERS + 1
    near = 8 + HALO
    rows = 2 * (near + HALO)

    def body(taps_ref, *refs):
        l_ref, r_ref, u_ref, w_ref, _, out_ref, pad_ref, edge_ref, sems = refs[-9:]

        def cut(top, plane, low):
            return jnp.concatenate([top, plane[:near], plane[LAT - near :], low], axis=0)

        def end(ref, side):
            return ref[count * HALO : (count + 1) * HALO, side * 128 : side * 128 + 128]

        left_ = cut(end(u_ref, 0), l_ref[...], end(w_ref, 0))
        right_ = cut(end(u_ref, 1), r_ref[...], end(w_ref, 1))
        for k, plane in enumerate(planes_of(refs[:-9])):
            at = pl.ds(k * HALO, HALO)
            pad_ref[k] = beside_lon(k, cut(u_ref[at], plane, w_ref[at]), left_, right_)
        for c in range(TRACERS):
            field = covariance(c, taps_ref, pad_ref, rows)
            done = (pad_ref[n + c, :, :LON])[None] * field[:, :, :LON]
            edge_ref[0, c] = done[:, HALO : HALO + 8]
            edge_ref[1, c] = done[:, rows - HALO - 8 : rows - HALO]
        copies = [
            pltpu.make_async_copy(
                edge_ref.at[e], out_ref.at[:, :, pl.ds(e * (LAT - 8), 8), :], sems.at[e]
            )
            for e in range(2)
        ]
        for copy in copies:
            copy.start()
        for copy in copies:
            copy.wait()

    operands = (*arrays, left, right, up, down)
    return pl.pallas_call(
        body,
        in_specs=[pl.BlockSpec(memory_space=pltpu.SMEM)]
        + [pl.BlockSpec(a.shape, lambda *_, d=a.ndim: (0,) * d) for a in operands]
        + [pl.BlockSpec(memory_space=pl.ANY)],
        out_specs=pl.BlockSpec(memory_space=pl.ANY),
        out_shape=jax.ShapeDtypeStruct(inner.shape, F32),
        input_output_aliases={len(operands) + 1: 0},
        scratch_shapes=[
            pltpu.VMEM((count, rows, PAD_LON), F32),
            pltpu.VMEM((2, TRACERS, TS_DEV, 8, LON), F32),
            pltpu.SemaphoreType.DMA((2,)),
        ],
        compiler_params=pltpu.CompilerParams(vmem_limit_bytes=12 * MIB),
        name="diffuse_edges",
    )(taps, *operands, inner)


def steps(axis, periodic):
    count = lax.axis_size(axis)
    forward = [(i, i + 1) for i in range(count - 1)]
    if periodic:
        forward.append((count - 1, 0))
    return forward, [(b, a) for a, b in forward]


def along_gy(parts):
    return [parts[0]] + [
        lax.ppermute(parts[k], "gy", [(i, (i + k) % N_GY) for i in range(N_GY)])
        for k in range(1, N_GY)
    ]


def along_gx(rows):
    return lax.all_to_all(
        rows.reshape(N_GX, rows.shape[0] // N_GX, HALF), "gx", 0, 0, tiled=True
    )


def per_device(residual, footprint, tile_id, step_id, block_id, sigma, taps, diffusivity):
    ids = (tile_id[:, 0], step_id, block_id)
    first_gx, first_gy = bin_sums(ids, residual.astype(F32), footprint)
    got_gx = along_gx(first_gx)
    some_gy = sum_arrays(along_gy(first_gy))
    all_gx = along_gy(sum_first(got_gx, N_GY))
    all_gy = along_gx(some_gy)
    adj, low, high = tile_sum(all_gx, all_gy)
    later, sooner = steps("ta", False)
    before = lax.ppermute(high, "ta", later)
    after = lax.ppermute(low, "ta", sooner)
    arrays = (before, adj, after, sigma, diffusivity[None])
    east, west = steps("gx", True)
    south, north = steps("gy", False)
    to_left, to_right = pack_lon(arrays, F32, "halo_lon")
    left = lax.ppermute(to_right, "gx", east)
    right = lax.ppermute(to_left, "gx", west)
    to_up, to_down = pack_lat(arrays, left, right, F32, "halo_lat")
    up = lax.ppermute(to_down, "gy", south)
    down = lax.ppermute(to_up, "gy", north)
    inner = diffuse_inner(arrays, left, right, taps)
    return diffuse_edges(inner, arrays, left, right, up, down, taps)


def solution(mesh):
    return jax.shard_map(
        per_device,
        mesh=mesh,
        in_specs=(
            P(("ta", "gy", "gx")),
            P(("ta", "gy", "gx"), None),
            P(("ta", "gy", "gx"), None),
            P(("ta", "gy", "gx")),
            P(("ta", "gy", "gx")),
            P(None, "gy", "gx"),
            P(),
            P("gy", "gx"),
        ),
        out_specs=P(None, "ta", "gy", "gx"),
        check_vma=False,
    )
```

```python
import jax
import jax.numpy as jnp
from jax import lax
from jax.experimental import pallas as pl
from jax.experimental.pallas import tpu as pltpu
from jax.sharding import PartitionSpec as P

TS_DEV = 4
TRACERS = 4
HB = 2
KSTEPS = 4
LAT = 64
LON = 256
FP = 1024
HALF = FP // 2
BINS = 64
SND = 2048
N_GY = 4
N_GX = 8
TILES = N_GY * N_GX
PAD_LAT = LAT + 16
PAD_LON = LON + 128
ROWS = BINS + 16
HALO = KSTEPS
F32 = jnp.float32
BF16 = jnp.bfloat16
MIB = 1 << 20


def bin_sums(ids, residual, footprint):
    rows = N_GX * BINS

    def body(tile_ref, step_ref, block_ref, res_ref, fp_ref, first_ref, *refs):
        sel_ref = refs[-1]
        c = pl.program_id(0)

        @pl.when(c == 0)
        def _():
            tile = tile_ref[...].reshape(1, SND)
            block = block_ref[...].reshape(1, SND)
            local = (block >> 1) * 8 + step_ref[...].reshape(1, SND) * 2 + (block & 1)
            away = (tile // N_GX - lax.axis_index("gy")) & (N_GY - 1)
            bins = ((away * N_GX + (tile & (N_GX - 1))) * BINS + local).astype(jnp.int16)
            weight = jnp.broadcast_to(res_ref[...].reshape(1, SND).astype(BF16), (16, SND))
            number = lax.broadcasted_iota(jnp.int32, (16, SND), 0).astype(jnp.int16)
            above = bins - number

            @pl.loop(0, TILES * BINS // 16, unroll=4)
            def _(m):
                hit = above == (m * 16).astype(jnp.int16)
                sel_ref[pl.ds(pl.multiple_of(m * 16, 16), 16), :] = jnp.where(
                    hit, weight, jnp.zeros((16, SND), BF16)
                )

        def sums(k):
            return jnp.dot(
                sel_ref[k * rows : (k + 1) * rows, :],
                fp_ref[...],
                preferred_element_type=F32,
            )

        @pl.when(c == 0)
        def _():
            for k in range(N_GY):
                out = sums(k).astype(BF16)
                for q in range(N_GX):
                    at = (q * N_GY + k) * BINS
                    first_ref[at : at + BINS, :] = out[q * BINS : (q + 1) * BINS]

        @pl.when(c == 1)
        def _():
            for k in range(N_GY):
                out = sums(k)
                refs[k][:rows, :] = out.astype(BF16)
                last = [out[(q + 1) * BINS - 8 : (q + 1) * BINS] for q in range(N_GX)]
                refs[(k + 1) % N_GY][rows:, :] = jnp.concatenate(last, axis=0).astype(BF16)

    one = pl.BlockSpec((SND,), lambda c: (0,))
    each = rows + N_GX * 8
    outs = pl.pallas_call(
        body,
        grid=(2,),
        in_specs=[one] * 4 + [pl.BlockSpec((SND, HALF), lambda c: (0, c))],
        out_specs=[pl.BlockSpec((TILES * BINS, HALF), lambda c: (0, 0))]
        + [pl.BlockSpec((each, HALF), lambda c: (0, 0))] * N_GY,
        out_shape=[jax.ShapeDtypeStruct((TILES * BINS, HALF), BF16)]
        + [jax.ShapeDtypeStruct((each, HALF), BF16)] * N_GY,
        scratch_shapes=[pltpu.VMEM((TILES * BINS, SND), BF16)],
        compiler_params=pltpu.CompilerParams(vmem_limit_bytes=58 * MIB),
        cost_estimate=pl.CostEstimate(
            flops=2 * TILES * BINS * SND * FP, bytes_accessed=8 * MIB, transcendentals=0
        ),
        name="bin_sums",
    )(*ids, residual, footprint)
    return outs[0], outs[1:]


def sum_first(got):
    count, rows, cols = got.shape

    def body(got_ref, *out_refs):
        totals = []
        for k in range(N_GY):
            at = pl.ds(k * BINS, BINS)
            total = got_ref[0, at].astype(F32)
            for s in range(1, count):
                total = total + got_ref[s, at].astype(F32)
            totals.append(total)
        none = jnp.zeros((8, cols), F32)
        for k, out_ref in enumerate(out_refs):
            below = totals[(k + 1) % N_GY][:8]
            out_ref[...] = jnp.concatenate([totals[k], below, none], axis=0).astype(BF16)

    return pl.pallas_call(
        body,
        out_shape=[jax.ShapeDtypeStruct((ROWS, cols), BF16)] * N_GY,
        compiler_params=pltpu.CompilerParams(vmem_limit_bytes=12 * MIB),
        name="sum_first",
    )(got)


def sum_arrays(arrays):
    cols = arrays[0].shape[1]

    def body(*refs):
        def total(at):
            out = refs[0][at].astype(F32)
            for ref in refs[1:-1]:
                out = out + ref[at].astype(F32)
            return out

        above = total(pl.ds(N_GX * BINS, N_GX * 8))
        none = jnp.zeros((8, cols), F32)
        for q in range(N_GX):
            halo = jnp.concatenate([above[q * 8 : q * 8 + 8], none], axis=0)
            refs[-1][q, :BINS] = total(pl.ds(q * BINS, BINS)).astype(BF16)
            refs[-1][q, BINS:] = halo.astype(BF16)

    return pl.pallas_call(
        body,
        out_shape=jax.ShapeDtypeStruct((N_GX, ROWS, cols), BF16),
        compiler_params=pltpu.CompilerParams(vmem_limit_bytes=12 * MIB),
        name="sum_arrays",
    )(*arrays)


def tile_sum(summed, got):
    count = got.shape[0]

    def body(*refs):
        got_ref, adj_ref, low_ref, high_ref, by_row = refs[-5:]
        first = refs[0][...].astype(F32)
        for ref in refs[1:-5]:
            first = first + ref[...].astype(F32)
        last = got_ref[0].astype(F32)
        for s in range(1, count):
            last = last + got_ref[s].astype(F32)
        by_row[...] = jnp.zeros_like(by_row)

        def put(row, part, at, i):
            by_row[pl.ds(row, 8, stride=PAD_LAT), :] = part[
                at : at + 8, i * 128 : i * 128 + 128
            ]

        for i in range(4):
            for br in range(8):
                put(8 + br * 8 + i, first, br * 8, i)
                put(8 + br * 8 + 4 + i, last, br * 8, i)
            put(4 + i, last, BINS, i)
            put(8 + LAT + i, first, BINS, i)
        for t in range(TS_DEV):
            for bc in range(2):
                at = (t * 2 + bc) * PAD_LAT
                adj_ref[t, :, bc * 128 : bc * 128 + 128] = by_row[at : at + PAD_LAT]
        low_ref[...] = adj_ref[:HB].astype(BF16)
        high_ref[...] = adj_ref[TS_DEV - HB :].astype(BF16)

    return pl.pallas_call(
        body,
        out_shape=[
            jax.ShapeDtypeStruct((TS_DEV, PAD_LAT, LON), F32),
            jax.ShapeDtypeStruct((HB, PAD_LAT, LON), BF16),
            jax.ShapeDtypeStruct((HB, PAD_LAT, LON), BF16),
        ],
        scratch_shapes=[pltpu.VMEM((TS_DEV * 2 * PAD_LAT, 128), F32)],
        compiler_params=pltpu.CompilerParams(vmem_limit_bytes=8 * MIB),
        name="tile_sum",
    )(*summed, got)


def put_strips(strip, dtype):
    rows = strip[0].shape[0]
    lane = lax.broadcasted_iota(jnp.int32, (rows, 128), 1)

    def packed(planes, side):
        out = jnp.zeros((rows, 128), F32)
        for k, plane in enumerate(planes):
            if side == 0:
                part = plane[:, :128]
                shift = HALO * k
            else:
                part = plane[:, LON - 128 :]
                shift = HALO * k + HALO
            moved = pltpu.roll(part, shift % 128, 1) if shift % 128 else part
            out = jnp.where((lane >= HALO * k) & (lane < HALO * k + HALO), moved, out)
        return out.astype(dtype)

    return packed(strip, 0), packed(strip, 1)


def pack_lon(arrays, dtype, name):
    counts = [a.shape[0] for a in arrays]

    def body(*refs):
        planes = [
            ref[k].astype(F32) for ref, count in zip(refs, counts) for k in range(count)
        ]
        refs[-2][...], refs[-1][...] = put_strips(planes, dtype)

    return pl.pallas_call(
        body,
        out_shape=[jax.ShapeDtypeStruct((arrays[0].shape[1], 128), dtype)] * 2,
        compiler_params=pltpu.CompilerParams(vmem_limit_bytes=8 * MIB),
        name=name,
    )(*arrays)


def pack_lat(arrays, from_left, from_right, dtype, name):
    counts = [a.shape[0] for a in arrays]
    n = sum(counts)

    def body(*refs):
        up_ref, down_ref = refs[-2:]
        strips = jnp.concatenate(
            [refs[-4][...].astype(F32), refs[-3][...].astype(F32)], axis=1
        )
        planes = [
            ref[k].astype(F32) for ref, count in zip(refs, counts) for k in range(count)
        ] + [strips]
        up = jnp.concatenate([p[:HALO] for p in planes], axis=0)
        down = jnp.concatenate([p[LAT - HALO :] for p in planes], axis=0)
        up_ref[...] = up.astype(dtype)
        down_ref[...] = down.astype(dtype)

    return pl.pallas_call(
        body,
        out_shape=[jax.ShapeDtypeStruct(((n + 1) * HALO, LON), dtype)] * 2,
        compiler_params=pltpu.CompilerParams(vmem_limit_bytes=8 * MIB),
        name=name,
    )(*arrays, from_left, from_right)


def beside_lon(k, plane, left, right):
    lane = lax.broadcasted_iota(jnp.int32, right.shape, 1)
    to_right = (-HALO * k) % 128
    to_left = (128 - HALO - HALO * k) % 128
    right = pltpu.roll(right, to_right, 1) if to_right else right
    left = pltpu.roll(left, to_left, 1) if to_left else left
    side = jnp.where(lane < HALO, right, jnp.where(lane >= 128 - HALO, left, 0.0))
    return jnp.concatenate([plane, side], axis=1)


def planes_of(refs):
    return [ref[k].astype(F32) for ref in refs for k in range(ref.shape[0])]


def pad_static(arrays, left, right, up, down):
    n = TRACERS + 1

    def body(*refs):
        l_ref, r_ref, u_ref, w_ref, out_ref = refs[-5:]
        none = [jnp.zeros((8 - HALO, 128), F32), jnp.zeros((8 - HALO, LON), F32)]

        def rows(top, mid, low):
            zero = none[mid.shape[1] // LON]
            return jnp.concatenate([zero, top, mid, low, zero], axis=0)

        def end(ref, side):
            return ref[n * HALO : (n + 1) * HALO, side * 128 : side * 128 + 128]

        left_ = rows(end(u_ref, 0), l_ref[...], end(w_ref, 0))
        right_ = rows(end(u_ref, 1), r_ref[...], end(w_ref, 1))
        for k, plane in enumerate(planes_of(refs[:-5])):
            at = pl.ds(k * HALO, HALO)
            out_ref[k] = beside_lon(k, rows(u_ref[at], plane, w_ref[at]), left_, right_)

    return pl.pallas_call(
        body,
        out_shape=jax.ShapeDtypeStruct((n, PAD_LAT, PAD_LON), F32),
        compiler_params=pltpu.CompilerParams(vmem_limit_bytes=8 * MIB),
        name="pad_static",
    )(*arrays, left, right, up, down)


def diffuse(arrays, left, right, static, taps):
    n = TS_DEV + 2 * HB

    def body(taps_ref, *refs):
        l_ref, r_ref, st_ref, out_ref, pad_ref = refs[-5:]
        c = pl.program_id(0)

        @pl.when(c == 0)
        def _():
            for k, plane in enumerate(planes_of(refs[:-5])):
                pad_ref[k] = beside_lon(k, plane, l_ref[...], r_ref[...])

        banded = taps_ref[c, 0] * pad_ref[0:TS_DEV]
        for k in range(1, 2 * HB + 1):
            banded = banded + taps_ref[c, k] * pad_ref[k : k + TS_DEV]
        field = st_ref[c][None] * banded
        rate = st_ref[TRACERS][None]
        for _ in range(KSTEPS):
            beside = (
                pltpu.roll(field, 1, 2)
                + pltpu.roll(field, PAD_LON - 1, 2)
                + pltpu.roll(field, 1, 1)
                + pltpu.roll(field, PAD_LAT - 1, 1)
            )
            field = field + rate * (beside - 4.0 * field)
        scale = st_ref[c, 8 : 8 + LAT, :LON]
        out_ref[0] = scale[None] * field[:, 8 : 8 + LAT, :LON]

    def whole(a):
        return pl.BlockSpec(a.shape, lambda c: (0,) * a.ndim)

    operands = (*arrays, left, right, static)
    return pl.pallas_call(
        body,
        grid=(TRACERS,),
        in_specs=[pl.BlockSpec(memory_space=pltpu.SMEM)] + [whole(a) for a in operands],
        out_specs=pl.BlockSpec((1, TS_DEV, LAT, LON), lambda c: (c, 0, 0, 0)),
        out_shape=jax.ShapeDtypeStruct((TRACERS, TS_DEV, LAT, LON), F32),
        scratch_shapes=[pltpu.VMEM((n, PAD_LAT, PAD_LON), F32)],
        compiler_params=pltpu.CompilerParams(vmem_limit_bytes=20 * MIB),
        name="diffuse",
    )(taps, *operands)


def steps(axis, periodic):
    count = lax.axis_size(axis)
    forward = [(i, i + 1) for i in range(count - 1)]
    if periodic:
        forward.append((count - 1, 0))
    return forward, [(b, a) for a, b in forward]


def along_gy(parts):
    return [parts[0]] + [
        lax.ppermute(parts[k], "gy", [(i, (i + k) % N_GY) for i in range(N_GY)])
        for k in range(1, N_GY)
    ]


def along_gx(rows):
    return lax.all_to_all(rows, "gx", 0, 0, tiled=True)


def per_device(residual, footprint, tile_id, step_id, block_id, sigma, taps, diffusivity):
    east, west = steps("gx", True)
    south, north = steps("gy", False)
    later, sooner = steps("ta", False)
    ids = (tile_id[:, 0], step_id, block_id)
    first_gx, first_gy = bin_sums(ids, residual, footprint)
    got_gx = along_gx(first_gx.reshape(N_GX, N_GY * BINS, HALF))
    came_gy = along_gy(first_gy)

    fixed = (sigma, diffusivity[None])
    fixed, first_gy = lax.optimization_barrier((fixed, first_gy))
    to_left, to_right = pack_lon(fixed, F32, "static_lon")
    left = lax.ppermute(to_right, "gx", east)
    right = lax.ppermute(to_left, "gx", west)
    to_up, to_down = pack_lat(fixed, left, right, F32, "static_lat")
    up = lax.ppermute(to_down, "gy", south)
    down = lax.ppermute(to_up, "gy", north)
    static = pad_static(fixed, left, right, up, down)
    static, came_gy = lax.optimization_barrier((static, came_gy))

    all_gx = along_gy(sum_first(got_gx))
    all_gy = along_gx(sum_arrays(came_gy))
    adj, low, high = tile_sum(all_gx, all_gy)
    before = lax.ppermute(high, "ta", later)
    after = lax.ppermute(low, "ta", sooner)
    arrays = (before, adj, after)
    to_left, to_right = pack_lon(arrays, F32, "adjoint_lon")
    left = lax.ppermute(to_right, "gx", east)
    right = lax.ppermute(to_left, "gx", west)
    return diffuse(arrays, left, right, static, taps)


def solution(mesh):
    return jax.shard_map(
        per_device,
        mesh=mesh,
        in_specs=(
            P(("ta", "gy", "gx")),
            P(("ta", "gy", "gx"), None),
            P(("ta", "gy", "gx"), None),
            P(("ta", "gy", "gx")),
            P(("ta", "gy", "gx")),
            P(None, "gy", "gx"),
            P(),
            P("gy", "gx"),
        ),
        out_specs=P(None, "ta", "gy", "gx"),
        check_vma=False,
    )
```

```python
import jax
import jax.numpy as jnp
from jax import lax
from jax.experimental import pallas as pl
from jax.experimental.pallas import tpu as pltpu
from jax.sharding import PartitionSpec as P

TS_DEV = 4
TRACERS = 4
HB = 2
KSTEPS = 4
LAT = 64
LON = 256
FP = 1024
HALF = FP // 2
BINS = 64
SND = 2048
N_GY = 4
N_GX = 8
TILES = N_GY * N_GX
PAD_LAT = LAT + 16
PAD_LON = LON + 128
ROWS = BINS + 16
HALO = KSTEPS
F32 = jnp.float32
BF16 = jnp.bfloat16
MIB = 1 << 20


def bin_sums(ids, residual, footprint):
    rows = N_GX * BINS

    def body(tile_ref, step_ref, block_ref, res_ref, fp_ref, first_ref, *refs):
        sel_ref = refs[-1]
        c = pl.program_id(0)

        @pl.when(c == 0)
        def _():
            tile = tile_ref[...].reshape(1, SND)
            block = block_ref[...].reshape(1, SND)
            local = (block >> 1) * 8 + step_ref[...].reshape(1, SND) * 2 + (block & 1)
            away = (tile // N_GX - lax.axis_index("gy")) & (N_GY - 1)
            bins = ((away * N_GX + (tile & (N_GX - 1))) * BINS + local).astype(jnp.int16)
            weight = jnp.broadcast_to(res_ref[...].reshape(1, SND).astype(BF16), (16, SND))
            number = lax.broadcasted_iota(jnp.int32, (16, SND), 0).astype(jnp.int16)
            above = bins - number

            @pl.loop(0, TILES * BINS // 16, unroll=4)
            def _(m):
                hit = above == (m * 16).astype(jnp.int16)
                sel_ref[pl.ds(pl.multiple_of(m * 16, 16), 16), :] = jnp.where(
                    hit, weight, jnp.zeros((16, SND), BF16)
                )

        def sums(k):
            return jnp.dot(
                sel_ref[k * rows : (k + 1) * rows, :],
                fp_ref[...],
                preferred_element_type=F32,
            )

        @pl.when(c == 0)
        def _():
            for k in range(N_GY):
                out = sums(k).astype(BF16)
                for q in range(N_GX):
                    at = (q * N_GY + k) * BINS
                    first_ref[at : at + BINS, :] = out[q * BINS : (q + 1) * BINS]

        @pl.when(c == 1)
        def _():
            for k in range(N_GY):
                out = sums(k)
                refs[k][:rows, :] = out.astype(BF16)
                last = [out[(q + 1) * BINS - 8 : (q + 1) * BINS] for q in range(N_GX)]
                refs[(k + 1) % N_GY][rows:, :] = jnp.concatenate(last, axis=0).astype(BF16)

    one = pl.BlockSpec((SND,), lambda c: (0,))
    each = rows + N_GX * 8
    outs = pl.pallas_call(
        body,
        grid=(2,),
        in_specs=[one] * 4 + [pl.BlockSpec((SND, HALF), lambda c: (0, c))],
        out_specs=[pl.BlockSpec((TILES * BINS, HALF), lambda c: (0, 0))]
        + [pl.BlockSpec((each, HALF), lambda c: (0, 0))] * N_GY,
        out_shape=[jax.ShapeDtypeStruct((TILES * BINS, HALF), BF16)]
        + [jax.ShapeDtypeStruct((each, HALF), BF16)] * N_GY,
        scratch_shapes=[pltpu.VMEM((TILES * BINS, SND), BF16)],
        compiler_params=pltpu.CompilerParams(vmem_limit_bytes=58 * MIB),
        cost_estimate=pl.CostEstimate(
            flops=2 * TILES * BINS * SND * FP, bytes_accessed=8 * MIB, transcendentals=0
        ),
        name="bin_sums",
    )(*ids, residual, footprint)
    return outs[0], outs[1:]


def sum_first(got):
    count, rows, cols = got.shape

    def body(got_ref, *out_refs):
        totals = []
        for k in range(N_GY):
            at = pl.ds(k * BINS, BINS)
            total = got_ref[0, at].astype(F32)
            for s in range(1, count):
                total = total + got_ref[s, at].astype(F32)
            totals.append(total)
        none = jnp.zeros((8, cols), F32)
        for k, out_ref in enumerate(out_refs):
            below = totals[(k + 1) % N_GY][:8]
            out_ref[...] = jnp.concatenate([totals[k], below, none], axis=0).astype(BF16)

    return pl.pallas_call(
        body,
        out_shape=[jax.ShapeDtypeStruct((ROWS, cols), BF16)] * N_GY,
        compiler_params=pltpu.CompilerParams(vmem_limit_bytes=12 * MIB),
        name="sum_first",
    )(got)


def sum_arrays(arrays):
    cols = arrays[0].shape[1]

    def body(*refs):
        def total(at):
            out = refs[0][at].astype(F32)
            for ref in refs[1:-1]:
                out = out + ref[at].astype(F32)
            return out

        above = total(pl.ds(N_GX * BINS, N_GX * 8))
        none = jnp.zeros((8, cols), F32)
        for q in range(N_GX):
            halo = jnp.concatenate([above[q * 8 : q * 8 + 8], none], axis=0)
            refs[-1][q, :BINS] = total(pl.ds(q * BINS, BINS)).astype(BF16)
            refs[-1][q, BINS:] = halo.astype(BF16)

    return pl.pallas_call(
        body,
        out_shape=jax.ShapeDtypeStruct((N_GX, ROWS, cols), BF16),
        compiler_params=pltpu.CompilerParams(vmem_limit_bytes=12 * MIB),
        name="sum_arrays",
    )(*arrays)


def tile_sum(summed, got):
    count = got.shape[0]

    def body(*refs):
        got_ref, adj_ref, low_ref, high_ref, by_row = refs[-5:]
        first = refs[0][...].astype(F32)
        for ref in refs[1:-5]:
            first = first + ref[...].astype(F32)
        last = got_ref[0].astype(F32)
        for s in range(1, count):
            last = last + got_ref[s].astype(F32)
        by_row[...] = jnp.zeros_like(by_row)

        def put(row, part, at, i):
            by_row[pl.ds(row, 8, stride=PAD_LAT), :] = part[
                at : at + 8, i * 128 : i * 128 + 128
            ]

        for i in range(4):
            for br in range(8):
                put(8 + br * 8 + i, first, br * 8, i)
                put(8 + br * 8 + 4 + i, last, br * 8, i)
            put(4 + i, last, BINS, i)
            put(8 + LAT + i, first, BINS, i)
        for t in range(TS_DEV):
            for bc in range(2):
                at = (t * 2 + bc) * PAD_LAT
                adj_ref[t, :, bc * 128 : bc * 128 + 128] = by_row[at : at + PAD_LAT]
        low_ref[...] = adj_ref[:HB].astype(BF16)
        high_ref[...] = adj_ref[TS_DEV - HB :].astype(BF16)

    return pl.pallas_call(
        body,
        out_shape=[
            jax.ShapeDtypeStruct((TS_DEV, PAD_LAT, LON), F32),
            jax.ShapeDtypeStruct((HB, PAD_LAT, LON), BF16),
            jax.ShapeDtypeStruct((HB, PAD_LAT, LON), BF16),
        ],
        scratch_shapes=[pltpu.VMEM((TS_DEV * 2 * PAD_LAT, 128), F32)],
        compiler_params=pltpu.CompilerParams(vmem_limit_bytes=8 * MIB),
        name="tile_sum",
    )(*summed, got)


def put_strips(strip, dtype):
    rows = strip[0].shape[0]
    lane = lax.broadcasted_iota(jnp.int32, (rows, 128), 1)

    def packed(planes, side):
        out = jnp.zeros((rows, 128), F32)
        for k, plane in enumerate(planes):
            if side == 0:
                part = plane[:, :128]
                shift = HALO * k
            else:
                part = plane[:, LON - 128 :]
                shift = HALO * k + HALO
            moved = pltpu.roll(part, shift % 128, 1) if shift % 128 else part
            out = jnp.where((lane >= HALO * k) & (lane < HALO * k + HALO), moved, out)
        return out.astype(dtype)

    return packed(strip, 0), packed(strip, 1)


def pack_lon(arrays, dtype, name):
    counts = [a.shape[0] for a in arrays]

    def body(*refs):
        planes = [
            ref[k].astype(F32) for ref, count in zip(refs, counts) for k in range(count)
        ]
        refs[-2][...], refs[-1][...] = put_strips(planes, dtype)

    return pl.pallas_call(
        body,
        out_shape=[jax.ShapeDtypeStruct((arrays[0].shape[1], 128), dtype)] * 2,
        compiler_params=pltpu.CompilerParams(vmem_limit_bytes=8 * MIB),
        name=name,
    )(*arrays)


def pack_rows(arrays):
    n = sum(a.shape[0] for a in arrays)

    def body(*refs):
        planes = planes_of(refs[:-2])
        refs[-2][...] = jnp.concatenate([p[:HALO] for p in planes], axis=0)
        refs[-1][...] = jnp.concatenate([p[LAT - HALO :] for p in planes], axis=0)

    return pl.pallas_call(
        body,
        out_shape=[jax.ShapeDtypeStruct((n * HALO, LON), F32)] * 2,
        compiler_params=pltpu.CompilerParams(vmem_limit_bytes=8 * MIB),
        name="static_rows",
    )(*arrays)


def beside_lat(arrays, up, down):
    n = sum(a.shape[0] for a in arrays)

    def body(*refs):
        u_ref, w_ref, out_ref = refs[-3:]
        zero = jnp.zeros((8 - HALO, LON), F32)
        for k, plane in enumerate(planes_of(refs[:-3])):
            at = pl.ds(k * HALO, HALO)
            out_ref[k] = jnp.concatenate([zero, u_ref[at], plane, w_ref[at], zero], axis=0)

    return pl.pallas_call(
        body,
        out_shape=jax.ShapeDtypeStruct((n, PAD_LAT, LON), F32),
        compiler_params=pltpu.CompilerParams(vmem_limit_bytes=8 * MIB),
        name="static_planes",
    )(*arrays, up, down)


def beside_lon(k, plane, left, right):
    lane = lax.broadcasted_iota(jnp.int32, right.shape, 1)
    to_right = (-HALO * k) % 128
    to_left = (128 - HALO - HALO * k) % 128
    right = pltpu.roll(right, to_right, 1) if to_right else right
    left = pltpu.roll(left, to_left, 1) if to_left else left
    side = jnp.where(lane < HALO, right, jnp.where(lane >= 128 - HALO, left, 0.0))
    return jnp.concatenate([plane, side], axis=1)


def planes_of(refs):
    return [ref[k].astype(F32) for ref in refs for k in range(ref.shape[0])]


def diffuse(arrays, left, right, taps):
    n = TS_DEV + 2 * HB

    def body(taps_ref, *refs):
        l_ref, r_ref, out_ref, pad_ref = refs[-4:]
        c = pl.program_id(0)

        @pl.when(c == 0)
        def _():
            for k, plane in enumerate(planes_of(refs[:-4])):
                pad_ref[k] = beside_lon(k, plane, l_ref[...], r_ref[...])

        banded = taps_ref[c, 0] * pad_ref[0:TS_DEV]
        for k in range(1, 2 * HB + 1):
            banded = banded + taps_ref[c, k] * pad_ref[k : k + TS_DEV]
        field = pad_ref[n + c][None] * banded
        rate = pad_ref[n + TRACERS][None]
        for _ in range(KSTEPS):
            beside = (
                pltpu.roll(field, 1, 2)
                + pltpu.roll(field, PAD_LON - 1, 2)
                + pltpu.roll(field, 1, 1)
                + pltpu.roll(field, PAD_LAT - 1, 1)
            )
            field = field + rate * (beside - 4.0 * field)
        scale = pad_ref[n + c, 8 : 8 + LAT, :LON]
        out_ref[0] = scale[None] * field[:, 8 : 8 + LAT, :LON]

    def whole(a):
        return pl.BlockSpec(a.shape, lambda c: (0,) * a.ndim)

    operands = (*arrays, left, right)
    return pl.pallas_call(
        body,
        grid=(TRACERS,),
        in_specs=[pl.BlockSpec(memory_space=pltpu.SMEM)] + [whole(a) for a in operands],
        out_specs=pl.BlockSpec((1, TS_DEV, LAT, LON), lambda c: (c, 0, 0, 0)),
        out_shape=jax.ShapeDtypeStruct((TRACERS, TS_DEV, LAT, LON), F32),
        scratch_shapes=[pltpu.VMEM((n + TRACERS + 1, PAD_LAT, PAD_LON), F32)],
        compiler_params=pltpu.CompilerParams(vmem_limit_bytes=20 * MIB),
        name="diffuse",
    )(taps, *operands)


def steps(axis, periodic):
    count = lax.axis_size(axis)
    forward = [(i, i + 1) for i in range(count - 1)]
    if periodic:
        forward.append((count - 1, 0))
    return forward, [(b, a) for a, b in forward]


def along_gy(parts):
    return [parts[0]] + [
        lax.ppermute(parts[k], "gy", [(i, (i + k) % N_GY) for i in range(N_GY)])
        for k in range(1, N_GY)
    ]


def along_gx(rows):
    return lax.all_to_all(rows, "gx", 0, 0, tiled=True)


def per_device(residual, footprint, tile_id, step_id, block_id, sigma, taps, diffusivity):
    east, west = steps("gx", True)
    south, north = steps("gy", False)
    later, sooner = steps("ta", False)
    ids = (tile_id[:, 0], step_id, block_id)
    first_gx, first_gy = bin_sums(ids, residual, footprint)
    got_gx = along_gx(first_gx.reshape(N_GX, N_GY * BINS, HALF))
    came_gy = along_gy(first_gy)

    fixed = (sigma, diffusivity[None])
    fixed, first_gy = lax.optimization_barrier((fixed, first_gy))
    to_up, to_down = pack_rows(fixed)
    up = lax.ppermute(to_down, "gy", south)
    down = lax.ppermute(to_up, "gy", north)
    static = beside_lat(fixed, up, down)

    parts = sum_first(got_gx)
    all_gx = along_gy(parts)
    came_gy, all_gx[0] = lax.optimization_barrier((came_gy, all_gx[0]))
    all_gy = along_gx(sum_arrays(came_gy))
    all_gx, static = lax.optimization_barrier((all_gx, static))
    adj, low, high = tile_sum(all_gx, all_gy)
    before = lax.ppermute(high, "ta", later)
    after = lax.ppermute(low, "ta", sooner)
    arrays = (before, adj, after, static)
    to_left, to_right = pack_lon(arrays, F32, "halo_lon")
    left = lax.ppermute(to_right, "gx", east)
    right = lax.ppermute(to_left, "gx", west)
    return diffuse(arrays, left, right, taps)


def solution(mesh):
    return jax.shard_map(
        per_device,
        mesh=mesh,
        in_specs=(
            P(("ta", "gy", "gx")),
            P(("ta", "gy", "gx"), None),
            P(("ta", "gy", "gx"), None),
            P(("ta", "gy", "gx")),
            P(("ta", "gy", "gx")),
            P(None, "gy", "gx"),
            P(),
            P("gy", "gx"),
        ),
        out_specs=P(None, "ta", "gy", "gx"),
        check_vma=False,
    )
```

```python
import jax
import jax.numpy as jnp
from jax import lax
from jax.experimental import pallas as pl
from jax.experimental.pallas import tpu as pltpu
from jax.sharding import PartitionSpec as P

TS_DEV = 4
TRACERS = 4
HB = 2
KSTEPS = 4
LAT = 64
LON = 256
FP = 1024
HALF = FP // 2
BINS = 64
SND = 2048
N_GY = 4
N_GX = 8
TILES = N_GY * N_GX
PAD_LAT = LAT + 16
PAD_LON = LON + 128
ROWS = BINS + 16
HALO = KSTEPS
F32 = jnp.float32
BF16 = jnp.bfloat16
MIB = 1 << 20


def bin_sums(ids, residual, footprint):
    rows = N_GX * BINS

    def body(tile_ref, step_ref, block_ref, res_ref, fp_ref, first_ref, *refs):
        sel_ref = refs[-1]
        c = pl.program_id(0)

        @pl.when(c == 0)
        def _():
            tile = tile_ref[...].reshape(1, SND)
            block = block_ref[...].reshape(1, SND)
            local = (block >> 1) * 8 + step_ref[...].reshape(1, SND) * 2 + (block & 1)
            away = (tile // N_GX - lax.axis_index("gy")) & (N_GY - 1)
            bins = ((away * N_GX + (tile & (N_GX - 1))) * BINS + local).astype(jnp.int16)
            weight = jnp.broadcast_to(res_ref[...].reshape(1, SND).astype(BF16), (16, SND))
            number = lax.broadcasted_iota(jnp.int32, (16, SND), 0).astype(jnp.int16)
            above = bins - number

            @pl.loop(0, TILES * BINS // 16, unroll=4)
            def _(m):
                hit = above == (m * 16).astype(jnp.int16)
                sel_ref[pl.ds(pl.multiple_of(m * 16, 16), 16), :] = jnp.where(
                    hit, weight, jnp.zeros((16, SND), BF16)
                )

        def sums(k):
            return jnp.dot(
                sel_ref[k * rows : (k + 1) * rows, :],
                fp_ref[...],
                preferred_element_type=F32,
            )

        @pl.when(c == 0)
        def _():
            for k in range(N_GY):
                out = sums(k).astype(BF16)
                for q in range(N_GX):
                    at = (q * N_GY + k) * BINS
                    first_ref[at : at + BINS, :] = out[q * BINS : (q + 1) * BINS]

        @pl.when(c == 1)
        def _():
            for k in range(N_GY):
                out = sums(k)
                refs[k][:rows, :] = out.astype(BF16)
                last = [out[(q + 1) * BINS - 8 : (q + 1) * BINS] for q in range(N_GX)]
                refs[(k + 1) % N_GY][rows:, :] = jnp.concatenate(last, axis=0).astype(BF16)

    one = pl.BlockSpec((SND,), lambda c: (0,))
    each = rows + N_GX * 8
    outs = pl.pallas_call(
        body,
        grid=(2,),
        in_specs=[one] * 4 + [pl.BlockSpec((SND, HALF), lambda c: (0, c))],
        out_specs=[pl.BlockSpec((TILES * BINS, HALF), lambda c: (0, 0))]
        + [pl.BlockSpec((each, HALF), lambda c: (0, 0))] * N_GY,
        out_shape=[jax.ShapeDtypeStruct((TILES * BINS, HALF), BF16)]
        + [jax.ShapeDtypeStruct((each, HALF), BF16)] * N_GY,
        scratch_shapes=[pltpu.VMEM((TILES * BINS, SND), BF16)],
        compiler_params=pltpu.CompilerParams(vmem_limit_bytes=58 * MIB),
        cost_estimate=pl.CostEstimate(
            flops=2 * TILES * BINS * SND * FP, bytes_accessed=8 * MIB, transcendentals=0
        ),
        name="bin_sums",
    )(*ids, residual, footprint)
    return outs[0], outs[1:]


def sum_first(got):
    count, rows, cols = got.shape

    def body(got_ref, *out_refs):
        totals = []
        for k in range(N_GY):
            at = pl.ds(k * BINS, BINS)
            total = got_ref[0, at].astype(F32)
            for s in range(1, count):
                total = total + got_ref[s, at].astype(F32)
            totals.append(total)
        none = jnp.zeros((8, cols), F32)
        for k, out_ref in enumerate(out_refs):
            below = totals[(k + 1) % N_GY][:8]
            out_ref[...] = jnp.concatenate([totals[k], below, none], axis=0).astype(BF16)

    return pl.pallas_call(
        body,
        out_shape=[jax.ShapeDtypeStruct((ROWS, cols), BF16)] * N_GY,
        compiler_params=pltpu.CompilerParams(vmem_limit_bytes=12 * MIB),
        name="sum_first",
    )(got)


def sum_arrays(arrays):
    cols = arrays[0].shape[1]

    def body(*refs):
        def total(at):
            out = refs[0][at].astype(F32)
            for ref in refs[1:-1]:
                out = out + ref[at].astype(F32)
            return out

        above = total(pl.ds(N_GX * BINS, N_GX * 8))
        none = jnp.zeros((8, cols), F32)
        for q in range(N_GX):
            halo = jnp.concatenate([above[q * 8 : q * 8 + 8], none], axis=0)
            refs[-1][q, :BINS] = total(pl.ds(q * BINS, BINS)).astype(BF16)
            refs[-1][q, BINS:] = halo.astype(BF16)

    return pl.pallas_call(
        body,
        out_shape=jax.ShapeDtypeStruct((N_GX, ROWS, cols), BF16),
        compiler_params=pltpu.CompilerParams(vmem_limit_bytes=12 * MIB),
        name="sum_arrays",
    )(*arrays)


def tile_sum(summed, got):
    count = got.shape[0]

    def body(*refs):
        got_ref, adj_ref, low_ref, high_ref, by_row = refs[-5:]
        first = refs[0][...].astype(F32)
        for ref in refs[1:-5]:
            first = first + ref[...].astype(F32)
        last = got_ref[0].astype(F32)
        for s in range(1, count):
            last = last + got_ref[s].astype(F32)
        by_row[...] = jnp.zeros_like(by_row)

        def put(row, part, at, i):
            by_row[pl.ds(row, 8, stride=PAD_LAT), :] = part[
                at : at + 8, i * 128 : i * 128 + 128
            ]

        for i in range(4):
            for br in range(8):
                put(8 + br * 8 + i, first, br * 8, i)
                put(8 + br * 8 + 4 + i, last, br * 8, i)
            put(4 + i, last, BINS, i)
            put(8 + LAT + i, first, BINS, i)
        for t in range(TS_DEV):
            for bc in range(2):
                at = (t * 2 + bc) * PAD_LAT
                adj_ref[t, :, bc * 128 : bc * 128 + 128] = by_row[at : at + PAD_LAT]
        low_ref[...] = adj_ref[:HB].astype(BF16)
        high_ref[...] = adj_ref[TS_DEV - HB :].astype(BF16)

    return pl.pallas_call(
        body,
        out_shape=[
            jax.ShapeDtypeStruct((TS_DEV, PAD_LAT, LON), F32),
            jax.ShapeDtypeStruct((HB, PAD_LAT, LON), BF16),
            jax.ShapeDtypeStruct((HB, PAD_LAT, LON), BF16),
        ],
        scratch_shapes=[pltpu.VMEM((TS_DEV * 2 * PAD_LAT, 128), F32)],
        compiler_params=pltpu.CompilerParams(vmem_limit_bytes=8 * MIB),
        name="tile_sum",
    )(*summed, got)


def put_strips(strip, dtype):
    rows = strip[0].shape[0]
    lane = lax.broadcasted_iota(jnp.int32, (rows, 128), 1)

    def packed(planes, side):
        out = jnp.zeros((rows, 128), F32)
        for k, plane in enumerate(planes):
            if side == 0:
                part = plane[:, :128]
                shift = HALO * k
            else:
                part = plane[:, LON - 128 :]
                shift = HALO * k + HALO
            moved = pltpu.roll(part, shift % 128, 1) if shift % 128 else part
            out = jnp.where((lane >= HALO * k) & (lane < HALO * k + HALO), moved, out)
        return out.astype(dtype)

    return packed(strip, 0), packed(strip, 1)


def pack_lon(arrays, dtype, name):
    counts = [a.shape[0] for a in arrays]

    def body(*refs):
        planes = [
            ref[k].astype(F32) for ref, count in zip(refs, counts) for k in range(count)
        ]
        refs[-2][...], refs[-1][...] = put_strips(planes, dtype)

    return pl.pallas_call(
        body,
        out_shape=[jax.ShapeDtypeStruct((arrays[0].shape[1], 128), dtype)] * 2,
        compiler_params=pltpu.CompilerParams(vmem_limit_bytes=8 * MIB),
        name=name,
    )(*arrays)


def pack_rows(arrays):
    n = sum(a.shape[0] for a in arrays)

    def body(*refs):
        planes = planes_of(refs[:-2])
        refs[-2][...] = jnp.concatenate([p[:HALO] for p in planes], axis=0)
        refs[-1][...] = jnp.concatenate([p[LAT - HALO :] for p in planes], axis=0)

    return pl.pallas_call(
        body,
        out_shape=[jax.ShapeDtypeStruct((n * HALO, LON), F32)] * 2,
        compiler_params=pltpu.CompilerParams(vmem_limit_bytes=8 * MIB),
        name="static_rows",
    )(*arrays)


def beside_lat(arrays, up, down):
    n = sum(a.shape[0] for a in arrays)

    def body(*refs):
        u_ref, w_ref, out_ref = refs[-3:]
        zero = jnp.zeros((8 - HALO, LON), F32)
        for k, plane in enumerate(planes_of(refs[:-3])):
            at = pl.ds(k * HALO, HALO)
            out_ref[k] = jnp.concatenate([zero, u_ref[at], plane, w_ref[at], zero], axis=0)

    return pl.pallas_call(
        body,
        out_shape=jax.ShapeDtypeStruct((n, PAD_LAT, LON), F32),
        compiler_params=pltpu.CompilerParams(vmem_limit_bytes=8 * MIB),
        name="static_planes",
    )(*arrays, up, down)


def beside_lon(k, plane, left, right):
    lane = lax.broadcasted_iota(jnp.int32, right.shape, 1)
    to_right = (-HALO * k) % 128
    to_left = (128 - HALO - HALO * k) % 128
    right = pltpu.roll(right, to_right, 1) if to_right else right
    left = pltpu.roll(left, to_left, 1) if to_left else left
    side = jnp.where(lane < HALO, right, jnp.where(lane >= 128 - HALO, left, 0.0))
    return jnp.concatenate([plane, side], axis=1)


def planes_of(refs):
    return [ref[k].astype(F32) for ref in refs for k in range(ref.shape[0])]


def diffuse(arrays, left, right, taps):
    n = TS_DEV + 2 * HB

    def body(taps_ref, *refs):
        l_ref, r_ref, out_ref, pad_ref = refs[-4:]
        c = pl.program_id(0)

        @pl.when(c == 0)
        def _():
            for k, plane in enumerate(planes_of(refs[:-4])):
                pad_ref[k] = beside_lon(k, plane, l_ref[...], r_ref[...])

        banded = taps_ref[c, 0] * pad_ref[0:TS_DEV]
        for k in range(1, 2 * HB + 1):
            banded = banded + taps_ref[c, k] * pad_ref[k : k + TS_DEV]
        field = pad_ref[n + c][None] * banded
        rate = pad_ref[n + TRACERS][None]
        for _ in range(KSTEPS):
            beside = (
                pltpu.roll(field, 1, 2)
                + pltpu.roll(field, PAD_LON - 1, 2)
                + pltpu.roll(field, 1, 1)
                + pltpu.roll(field, PAD_LAT - 1, 1)
            )
            field = field + rate * (beside - 4.0 * field)
        scale = pad_ref[n + c, 8 : 8 + LAT, :LON]
        out_ref[0] = scale[None] * field[:, 8 : 8 + LAT, :LON]

    def whole(a):
        return pl.BlockSpec(a.shape, lambda c: (0,) * a.ndim)

    operands = (*arrays, left, right)
    return pl.pallas_call(
        body,
        grid=(TRACERS,),
        in_specs=[pl.BlockSpec(memory_space=pltpu.SMEM)] + [whole(a) for a in operands],
        out_specs=pl.BlockSpec((1, TS_DEV, LAT, LON), lambda c: (c, 0, 0, 0)),
        out_shape=jax.ShapeDtypeStruct((TRACERS, TS_DEV, LAT, LON), F32),
        scratch_shapes=[pltpu.VMEM((n + TRACERS + 1, PAD_LAT, PAD_LON), F32)],
        compiler_params=pltpu.CompilerParams(vmem_limit_bytes=20 * MIB),
        name="diffuse",
    )(taps, *operands)


def steps(axis, periodic):
    count = lax.axis_size(axis)
    forward = [(i, i + 1) for i in range(count - 1)]
    if periodic:
        forward.append((count - 1, 0))
    return forward, [(b, a) for a, b in forward]


def along_gy(parts):
    return [parts[0]] + [
        lax.ppermute(parts[k], "gy", [(i, (i + k) % N_GY) for i in range(N_GY)])
        for k in range(1, N_GY)
    ]


def along_gx(rows):
    return lax.all_to_all(rows, "gx", 0, 0, tiled=True)


def per_device(residual, footprint, tile_id, step_id, block_id, sigma, taps, diffusivity):
    east, west = steps("gx", True)
    south, north = steps("gy", False)
    later, sooner = steps("ta", False)
    ids = (tile_id[:, 0], step_id, block_id)
    first_gx, first_gy = bin_sums(ids, residual, footprint)
    got_gx = along_gx(first_gx.reshape(N_GX, N_GY * BINS, HALF))
    came_gy = along_gy(first_gy)

    fixed = (sigma, diffusivity[None])
    fixed, first_gy = lax.optimization_barrier((fixed, first_gy))
    to_up, to_down = pack_rows(fixed)
    up = lax.ppermute(to_down, "gy", south)
    down = lax.ppermute(to_up, "gy", north)
    came_gy, up, down = lax.optimization_barrier((came_gy, up, down))
    static = beside_lat(fixed, up, down)

    all_gx = along_gy(sum_first(got_gx))
    all_gy = along_gx(sum_arrays(came_gy))
    adj, low, high = tile_sum(all_gx, all_gy)
    before = lax.ppermute(high, "ta", later)
    after = lax.ppermute(low, "ta", sooner)
    arrays = (before, adj, after, static)
    to_left, to_right = pack_lon(arrays, F32, "halo_lon")
    left = lax.ppermute(to_right, "gx", east)
    right = lax.ppermute(to_left, "gx", west)
    return diffuse(arrays, left, right, taps)


def solution(mesh):
    return jax.shard_map(
        per_device,
        mesh=mesh,
        in_specs=(
            P(("ta", "gy", "gx")),
            P(("ta", "gy", "gx"), None),
            P(("ta", "gy", "gx"), None),
            P(("ta", "gy", "gx")),
            P(("ta", "gy", "gx")),
            P(None, "gy", "gx"),
            P(),
            P("gy", "gx"),
        ),
        out_specs=P(None, "ta", "gy", "gx"),
        check_vma=False,
    )
```

```python
import jax
import jax.numpy as jnp
from jax import lax
from jax.experimental import pallas as pl
from jax.experimental.pallas import tpu as pltpu
from jax.sharding import PartitionSpec as P

TS_DEV = 4
TRACERS = 4
HB = 2
KSTEPS = 4
LAT = 64
LON = 256
FP = 1024
HALF = FP // 2
BINS = 64
SND = 2048
N_GY = 4
N_GX = 8
TILES = N_GY * N_GX
PAD_LAT = LAT + 16
PAD_LON = LON + 128
ROWS = BINS + 16
HALO = KSTEPS
F32 = jnp.float32
BF16 = jnp.bfloat16
MIB = 1 << 20


def bin_sums(ids, residual, footprint):
    rows = N_GX * BINS
    most = BINS - 8

    def body(tile_ref, step_ref, block_ref, res_ref, fp_ref, first_ref, *refs):
        fp_buf, sel_ref, first_buf, second_buf, in_sems, first_sems, second_sems = refs[N_GY:]
        loads = [
            pltpu.make_async_copy(
                fp_ref.at[:, pl.ds(h * HALF, HALF)], fp_buf.at[h], in_sems.at[h]
            )
            for h in range(2)
        ]
        for load in loads:
            load.start()
        tile = tile_ref[...].reshape(1, SND)
        block = block_ref[...].reshape(1, SND)
        local = (block >> 1) * 8 + step_ref[...].reshape(1, SND) * 2 + (block & 1)
        away = (tile // N_GX - lax.axis_index("gy")) & (N_GY - 1)
        bins = ((away * N_GX + (tile & (N_GX - 1))) * BINS + local).astype(jnp.int16)
        weight = jnp.broadcast_to(res_ref[...].reshape(1, SND).astype(BF16), (16, SND))
        above = bins - lax.broadcasted_iota(jnp.int32, (16, SND), 0).astype(jnp.int16)

        @pl.loop(0, TILES * BINS // 16, unroll=4)
        def _(m):
            hit = above == (m * 16).astype(jnp.int16)
            sel_ref[pl.ds(pl.multiple_of(m * 16, 16), 16), :] = jnp.where(
                hit, weight, jnp.zeros((16, SND), BF16)
            )

        for load in loads:
            load.wait()
        stores = []
        for k in range(N_GY):
            halves = [
                jnp.dot(
                    sel_ref[k * rows : (k + 1) * rows, :],
                    fp_buf[h],
                    preferred_element_type=F32,
                ).reshape(N_GX, BINS, HALF)
                for h in range(2)
            ]
            for h, buf in enumerate((first_buf, second_buf)):
                both = [halves[h][:, :most], halves[1 - h][:, most:]]
                buf[k] = jnp.concatenate(both, axis=1).astype(BF16)
            stores += [
                pltpu.make_async_copy(
                    first_buf.at[k],
                    first_ref.at[:, pl.ds(k * BINS, BINS), :],
                    first_sems.at[k],
                ),
                pltpu.make_async_copy(second_buf.at[k], refs[k], second_sems.at[k]),
            ]
            stores[-2].start()
            stores[-1].start()
        for store in stores:
            store.wait()

    one = pl.BlockSpec((SND,), lambda: (0,))
    far = pl.BlockSpec(memory_space=pl.ANY)
    outs = pl.pallas_call(
        body,
        in_specs=[one] * 4 + [far],
        out_specs=[far] * (1 + N_GY),
        out_shape=[jax.ShapeDtypeStruct((N_GX, N_GY * BINS, HALF), BF16)]
        + [jax.ShapeDtypeStruct((N_GX, BINS, HALF), BF16)] * N_GY,
        scratch_shapes=[
            pltpu.VMEM((2, SND, HALF), BF16),
            pltpu.VMEM((TILES * BINS, SND), BF16),
            pltpu.VMEM((N_GY, N_GX, BINS, HALF), BF16),
            pltpu.VMEM((N_GY, N_GX, BINS, HALF), BF16),
            pltpu.SemaphoreType.DMA((2,)),
            pltpu.SemaphoreType.DMA((N_GY,)),
            pltpu.SemaphoreType.DMA((N_GY,)),
        ],
        compiler_params=pltpu.CompilerParams(vmem_limit_bytes=58 * MIB),
        cost_estimate=pl.CostEstimate(
            flops=2 * TILES * BINS * SND * FP, bytes_accessed=8 * MIB, transcendentals=0
        ),
        name="bin_sums",
    )(*ids, residual, footprint)
    return outs[0], outs[1:]


def sum_first(got):
    count, rows, cols = got.shape

    def body(got_ref, *out_refs):
        totals = []
        for k in range(N_GY):
            at = pl.ds(k * BINS, BINS)
            total = got_ref[0, at].astype(F32)
            for s in range(1, count):
                total = total + got_ref[s, at].astype(F32)
            totals.append(total)
        for k, out_ref in enumerate(out_refs):
            below = totals[(k + 1) % N_GY][:8]
            over = totals[(k - 1) % N_GY][BINS - 8 :]
            out_ref[...] = jnp.concatenate([totals[k], below, over], axis=0).astype(BF16)

    return pl.pallas_call(
        body,
        out_shape=[jax.ShapeDtypeStruct((ROWS, cols), BF16)] * N_GY,
        compiler_params=pltpu.CompilerParams(vmem_limit_bytes=12 * MIB),
        name="sum_first",
    )(got)


def sum_arrays(arrays):
    def body(*refs):
        for q in range(N_GX):
            total = refs[0][q].astype(F32)
            for ref in refs[1:-1]:
                total = total + ref[q].astype(F32)
            refs[-1][q] = total.astype(BF16)

    return pl.pallas_call(
        body,
        out_shape=jax.ShapeDtypeStruct(arrays[0].shape, BF16),
        compiler_params=pltpu.CompilerParams(vmem_limit_bytes=12 * MIB),
        name="sum_arrays",
    )(*arrays)


def tile_sum(summed, got):
    count = got.shape[0]

    def body(*refs):
        got_ref, adj_ref, low_ref, high_ref, by_row = refs[-5:]
        first = refs[0][...].astype(F32)
        for ref in refs[1:-5]:
            first = first + ref[...].astype(F32)
        last = got_ref[0].astype(F32)
        for s in range(1, count):
            last = last + got_ref[s].astype(F32)
        by_row[...] = jnp.zeros_like(by_row)

        def put(row, part, at, i):
            by_row[pl.ds(row, 8, stride=PAD_LAT), :] = part[
                at : at + 8, i * 128 : i * 128 + 128
            ]

        for i in range(4):
            for br in range(7):
                put(8 + br * 8 + i, first, br * 8, i)
                put(8 + br * 8 + 4 + i, last, br * 8, i)
            put(LAT + i, last, BINS - 8, i)
            put(LAT + 4 + i, first, BINS - 8, i)
            put(8 + LAT + i, first, BINS, i)
            put(4 + i, first, BINS + 8, i)
        for t in range(TS_DEV):
            for bc in range(2):
                at = (t * 2 + bc) * PAD_LAT
                adj_ref[t, :, bc * 128 : bc * 128 + 128] = by_row[at : at + PAD_LAT]
        low_ref[...] = adj_ref[:HB].astype(BF16)
        high_ref[...] = adj_ref[TS_DEV - HB :].astype(BF16)

    return pl.pallas_call(
        body,
        out_shape=[
            jax.ShapeDtypeStruct((TS_DEV, PAD_LAT, LON), F32),
            jax.ShapeDtypeStruct((HB, PAD_LAT, LON), BF16),
            jax.ShapeDtypeStruct((HB, PAD_LAT, LON), BF16),
        ],
        scratch_shapes=[pltpu.VMEM((TS_DEV * 2 * PAD_LAT, 128), F32)],
        compiler_params=pltpu.CompilerParams(vmem_limit_bytes=8 * MIB),
        name="tile_sum",
    )(*summed, got)


def put_strips(strip, dtype):
    rows = strip[0].shape[0]
    lane = lax.broadcasted_iota(jnp.int32, (rows, 128), 1)

    def packed(planes, side):
        out = jnp.zeros((rows, 128), F32)
        for k, plane in enumerate(planes):
            if side == 0:
                part = plane[:, :128]
                shift = HALO * k
            else:
                part = plane[:, LON - 128 :]
                shift = HALO * k + HALO
            moved = pltpu.roll(part, shift % 128, 1) if shift % 128 else part
            out = jnp.where((lane >= HALO * k) & (lane < HALO * k + HALO), moved, out)
        return out.astype(dtype)

    return packed(strip, 0), packed(strip, 1)


def pack_lon(arrays, dtype, name):
    counts = [a.shape[0] for a in arrays]

    def body(*refs):
        planes = [
            ref[k].astype(F32) for ref, count in zip(refs, counts) for k in range(count)
        ]
        refs[-2][...], refs[-1][...] = put_strips(planes, dtype)

    return pl.pallas_call(
        body,
        out_shape=[jax.ShapeDtypeStruct((arrays[0].shape[1], 128), dtype)] * 2,
        compiler_params=pltpu.CompilerParams(vmem_limit_bytes=8 * MIB),
        name=name,
    )(*arrays)


def pack_rows(arrays):
    n = sum(a.shape[0] for a in arrays)

    def body(*refs):
        planes = planes_of(refs[:-2])
        refs[-2][...] = jnp.concatenate([p[:HALO] for p in planes], axis=0)
        refs[-1][...] = jnp.concatenate([p[LAT - HALO :] for p in planes], axis=0)

    return pl.pallas_call(
        body,
        out_shape=[jax.ShapeDtypeStruct((n * HALO, LON), F32)] * 2,
        compiler_params=pltpu.CompilerParams(vmem_limit_bytes=8 * MIB),
        name="static_rows",
    )(*arrays)


def beside_lat(arrays, up, down):
    n = sum(a.shape[0] for a in arrays)

    def body(*refs):
        u_ref, w_ref, out_ref = refs[-3:]
        zero = jnp.zeros((8 - HALO, LON), F32)
        for k, plane in enumerate(planes_of(refs[:-3])):
            at = pl.ds(k * HALO, HALO)
            out_ref[k] = jnp.concatenate([zero, u_ref[at], plane, w_ref[at], zero], axis=0)

    return pl.pallas_call(
        body,
        out_shape=jax.ShapeDtypeStruct((n, PAD_LAT, LON), F32),
        compiler_params=pltpu.CompilerParams(vmem_limit_bytes=8 * MIB),
        name="static_planes",
    )(*arrays, up, down)


def beside_lon(k, plane, left, right):
    lane = lax.broadcasted_iota(jnp.int32, right.shape, 1)
    to_right = (-HALO * k) % 128
    to_left = (128 - HALO - HALO * k) % 128
    right = pltpu.roll(right, to_right, 1) if to_right else right
    left = pltpu.roll(left, to_left, 1) if to_left else left
    side = jnp.where(lane < HALO, right, jnp.where(lane >= 128 - HALO, left, 0.0))
    return jnp.concatenate([plane, side], axis=1)


def planes_of(refs):
    return [ref[k].astype(F32) for ref in refs for k in range(ref.shape[0])]


def diffuse(arrays, left, right, taps):
    n = TS_DEV + 2 * HB

    def body(taps_ref, *refs):
        l_ref, r_ref, out_ref, pad_ref = refs[-4:]
        c = pl.program_id(0)

        @pl.when(c == 0)
        def _():
            for k, plane in enumerate(planes_of(refs[:-4])):
                pad_ref[k] = beside_lon(k, plane, l_ref[...], r_ref[...])

        banded = taps_ref[c, 0] * pad_ref[0:TS_DEV]
        for k in range(1, 2 * HB + 1):
            banded = banded + taps_ref[c, k] * pad_ref[k : k + TS_DEV]
        field = pad_ref[n + c][None] * banded
        rate = pad_ref[n + TRACERS][None]
        for _ in range(KSTEPS):
            beside = (
                pltpu.roll(field, 1, 2)
                + pltpu.roll(field, PAD_LON - 1, 2)
                + pltpu.roll(field, 1, 1)
                + pltpu.roll(field, PAD_LAT - 1, 1)
            )
            field = field + rate * (beside - 4.0 * field)
        scale = pad_ref[n + c, 8 : 8 + LAT, :LON]
        out_ref[0] = scale[None] * field[:, 8 : 8 + LAT, :LON]

    def whole(a):
        return pl.BlockSpec(a.shape, lambda c: (0,) * a.ndim)

    operands = (*arrays, left, right)
    return pl.pallas_call(
        body,
        grid=(TRACERS,),
        in_specs=[pl.BlockSpec(memory_space=pltpu.SMEM)] + [whole(a) for a in operands],
        out_specs=pl.BlockSpec((1, TS_DEV, LAT, LON), lambda c: (c, 0, 0, 0)),
        out_shape=jax.ShapeDtypeStruct((TRACERS, TS_DEV, LAT, LON), F32),
        scratch_shapes=[pltpu.VMEM((n + TRACERS + 1, PAD_LAT, PAD_LON), F32)],
        compiler_params=pltpu.CompilerParams(vmem_limit_bytes=20 * MIB),
        name="diffuse",
    )(taps, *operands)


def steps(axis, periodic):
    count = lax.axis_size(axis)
    forward = [(i, i + 1) for i in range(count - 1)]
    if periodic:
        forward.append((count - 1, 0))
    return forward, [(b, a) for a, b in forward]


def along_gy(parts):
    return [parts[0]] + [
        lax.ppermute(parts[k], "gy", [(i, (i + k) % N_GY) for i in range(N_GY)])
        for k in range(1, N_GY)
    ]


def along_gx(rows):
    return lax.all_to_all(rows, "gx", 0, 0, tiled=True)


def per_device(residual, footprint, tile_id, step_id, block_id, sigma, taps, diffusivity):
    east, west = steps("gx", True)
    south, north = steps("gy", False)
    later, sooner = steps("ta", False)
    ids = (tile_id[:, 0], step_id, block_id)
    first_gx, first_gy = bin_sums(ids, residual, footprint)
    got_gx = along_gx(first_gx)
    came_gy = along_gy(first_gy)

    fixed = (sigma, diffusivity[None])
    fixed, first_gy = lax.optimization_barrier((fixed, first_gy))
    to_up, to_down = pack_rows(fixed)
    up = lax.ppermute(to_down, "gy", south)
    down = lax.ppermute(to_up, "gy", north)
    came_gy, up, down = lax.optimization_barrier((came_gy, up, down))
    static = beside_lat(fixed, up, down)

    all_gx = along_gy(sum_first(got_gx))
    all_gy = along_gx(sum_arrays(came_gy))
    adj, low, high = tile_sum(all_gx, all_gy)
    before = lax.ppermute(high, "ta", later)
    after = lax.ppermute(low, "ta", sooner)
    arrays = (before, adj, after, static)
    to_left, to_right = pack_lon(arrays, F32, "halo_lon")
    left = lax.ppermute(to_right, "gx", east)
    right = lax.ppermute(to_left, "gx", west)
    return diffuse(arrays, left, right, taps)


def solution(mesh):
    return jax.shard_map(
        per_device,
        mesh=mesh,
        in_specs=(
            P(("ta", "gy", "gx")),
            P(("ta", "gy", "gx"), None),
            P(("ta", "gy", "gx"), None),
            P(("ta", "gy", "gx")),
            P(("ta", "gy", "gx")),
            P(None, "gy", "gx"),
            P(),
            P("gy", "gx"),
        ),
        out_specs=P(None, "ta", "gy", "gx"),
        check_vma=False,
    )
```

```python
import jax
import jax.numpy as jnp
from jax import lax
from jax.experimental import pallas as pl
from jax.experimental.pallas import tpu as pltpu
from jax.sharding import PartitionSpec as P

TS_DEV = 4
TRACERS = 4
HB = 2
KSTEPS = 4
LAT = 64
LON = 256
FP = 1024
HALF = FP // 2
BINS = 64
SND = 2048
N_GY = 4
N_GX = 8
TILES = N_GY * N_GX
PAD_LAT = LAT + 16
PAD_LON = LON + 128
ROWS = BINS + 16
HALO = KSTEPS
F32 = jnp.float32
BF16 = jnp.bfloat16
MIB = 1 << 20


def bin_sums(ids, residual, footprint):
    rows = N_GX * BINS
    most = BINS - 8

    def body(tile_ref, step_ref, block_ref, res_ref, fp_ref, first_ref, *refs):
        fp_buf, sel_ref, first_buf, second_buf, in_sems, first_sems, second_sems = refs[N_GY:]
        loads = [
            pltpu.make_async_copy(
                fp_ref.at[:, pl.ds(h * HALF, HALF)], fp_buf.at[h], in_sems.at[h]
            )
            for h in range(2)
        ]
        for load in loads:
            load.start()
        tile = tile_ref[...].reshape(1, SND)
        block = block_ref[...].reshape(1, SND)
        local = (block >> 1) * 8 + step_ref[...].reshape(1, SND) * 2 + (block & 1)
        away = (tile // N_GX - lax.axis_index("gy")) & (N_GY - 1)
        bins = ((away * N_GX + (tile & (N_GX - 1))) * BINS + local).astype(jnp.int16)
        weight = jnp.broadcast_to(res_ref[...].reshape(1, SND).astype(BF16), (16, SND))
        above = bins - lax.broadcasted_iota(jnp.int32, (16, SND), 0).astype(jnp.int16)

        @pl.loop(0, TILES * BINS // 16, unroll=4)
        def _(m):
            hit = above == (m * 16).astype(jnp.int16)
            sel_ref[pl.ds(pl.multiple_of(m * 16, 16), 16), :] = jnp.where(
                hit, weight, jnp.zeros((16, SND), BF16)
            )

        for load in loads:
            load.wait()
        stores = []
        for k in range(N_GY):
            halves = [
                jnp.dot(
                    sel_ref[k * rows : (k + 1) * rows, :],
                    fp_buf[h],
                    preferred_element_type=F32,
                ).reshape(N_GX, BINS, HALF)
                for h in range(2)
            ]
            for h, buf in enumerate((first_buf, second_buf)):
                both = [halves[h][:, :most], halves[1 - h][:, most:]]
                buf[k] = jnp.concatenate(both, axis=1).astype(BF16)
            stores += [
                pltpu.make_async_copy(
                    first_buf.at[k],
                    first_ref.at[:, pl.ds(k * BINS, BINS), :],
                    first_sems.at[k],
                ),
                pltpu.make_async_copy(second_buf.at[k], refs[k], second_sems.at[k]),
            ]
            stores[-2].start()
            stores[-1].start()
        for store in stores:
            store.wait()

    one = pl.BlockSpec((SND,), lambda: (0,))
    far = pl.BlockSpec(memory_space=pl.ANY)
    outs = pl.pallas_call(
        body,
        in_specs=[one] * 4 + [far],
        out_specs=[far] * (1 + N_GY),
        out_shape=[jax.ShapeDtypeStruct((N_GX, N_GY * BINS, HALF), BF16)]
        + [jax.ShapeDtypeStruct((N_GX, BINS, HALF), BF16)] * N_GY,
        scratch_shapes=[
            pltpu.VMEM((2, SND, HALF), BF16),
            pltpu.VMEM((TILES * BINS, SND), BF16),
            pltpu.VMEM((N_GY, N_GX, BINS, HALF), BF16),
            pltpu.VMEM((N_GY, N_GX, BINS, HALF), BF16),
            pltpu.SemaphoreType.DMA((2,)),
            pltpu.SemaphoreType.DMA((N_GY,)),
            pltpu.SemaphoreType.DMA((N_GY,)),
        ],
        compiler_params=pltpu.CompilerParams(vmem_limit_bytes=58 * MIB),
        cost_estimate=pl.CostEstimate(
            flops=2 * TILES * BINS * SND * FP, bytes_accessed=8 * MIB, transcendentals=0
        ),
        name="bin_sums",
    )(*ids, residual, footprint)
    return outs[0], outs[1:]


def sum_first(got):
    count, rows, cols = got.shape

    def body(got_ref, *out_refs):
        totals = []
        for k in range(N_GY):
            at = pl.ds(k * BINS, BINS)
            total = got_ref[0, at].astype(F32)
            for s in range(1, count):
                total = total + got_ref[s, at].astype(F32)
            totals.append(total)
        for k, out_ref in enumerate(out_refs):
            below = totals[(k + 1) % N_GY][:8]
            over = totals[(k - 1) % N_GY][BINS - 8 :]
            out_ref[...] = jnp.concatenate([totals[k], below, over], axis=0).astype(BF16)

    return pl.pallas_call(
        body,
        out_shape=[jax.ShapeDtypeStruct((ROWS, cols), BF16)] * N_GY,
        compiler_params=pltpu.CompilerParams(vmem_limit_bytes=12 * MIB),
        name="sum_first",
    )(got)


def sum_arrays(arrays):
    def body(*refs):
        for q in range(N_GX):
            total = refs[0][q].astype(F32)
            for ref in refs[1:-1]:
                total = total + ref[q].astype(F32)
            refs[-1][q] = total.astype(BF16)

    return pl.pallas_call(
        body,
        out_shape=jax.ShapeDtypeStruct(arrays[0].shape, BF16),
        compiler_params=pltpu.CompilerParams(vmem_limit_bytes=12 * MIB),
        name="sum_arrays",
    )(*arrays)


def tile_sum(summed, got):
    count = got.shape[0]

    def body(*refs):
        got_ref, adj_ref, low_ref, high_ref, by_row = refs[-5:]
        first = refs[0][...].astype(F32)
        for ref in refs[1:-5]:
            first = first + ref[...].astype(F32)
        last = got_ref[0].astype(F32)
        for s in range(1, count):
            last = last + got_ref[s].astype(F32)
        by_row[...] = jnp.zeros_like(by_row)

        def put(row, part, at, i):
            by_row[pl.ds(row, 8, stride=PAD_LAT), :] = part[
                at : at + 8, i * 128 : i * 128 + 128
            ]

        for i in range(4):
            for br in range(7):
                put(8 + br * 8 + i, first, br * 8, i)
                put(8 + br * 8 + 4 + i, last, br * 8, i)
            put(LAT + i, last, BINS - 8, i)
            put(LAT + 4 + i, first, BINS - 8, i)
            put(8 + LAT + i, first, BINS, i)
            put(4 + i, first, BINS + 8, i)
        for t in range(TS_DEV):
            for bc in range(2):
                at = (t * 2 + bc) * PAD_LAT
                adj_ref[t, :, bc * 128 : bc * 128 + 128] = by_row[at : at + PAD_LAT]
        low_ref[...] = adj_ref[:HB].astype(BF16)
        high_ref[...] = adj_ref[TS_DEV - HB :].astype(BF16)

    return pl.pallas_call(
        body,
        out_shape=[
            jax.ShapeDtypeStruct((TS_DEV, PAD_LAT, LON), F32),
            jax.ShapeDtypeStruct((HB, PAD_LAT, LON), BF16),
            jax.ShapeDtypeStruct((HB, PAD_LAT, LON), BF16),
        ],
        scratch_shapes=[pltpu.VMEM((TS_DEV * 2 * PAD_LAT, 128), F32)],
        compiler_params=pltpu.CompilerParams(vmem_limit_bytes=8 * MIB),
        name="tile_sum",
    )(*summed, got)


def put_strips(strip, dtype):
    rows = strip[0].shape[0]
    lane = lax.broadcasted_iota(jnp.int32, (rows, 128), 1)

    def packed(planes, side):
        out = jnp.zeros((rows, 128), F32)
        for k, plane in enumerate(planes):
            if side == 0:
                part = plane[:, :128]
                shift = HALO * k
            else:
                part = plane[:, LON - 128 :]
                shift = HALO * k + HALO
            moved = pltpu.roll(part, shift % 128, 1) if shift % 128 else part
            out = jnp.where((lane >= HALO * k) & (lane < HALO * k + HALO), moved, out)
        return out.astype(dtype)

    return packed(strip, 0), packed(strip, 1)


def pack_lon(arrays, dtype, name):
    counts = [a.shape[0] for a in arrays]

    def body(*refs):
        planes = [
            ref[k].astype(F32) for ref, count in zip(refs, counts) for k in range(count)
        ]
        refs[-2][...], refs[-1][...] = put_strips(planes, dtype)

    return pl.pallas_call(
        body,
        out_shape=[jax.ShapeDtypeStruct((arrays[0].shape[1], 128), dtype)] * 2,
        compiler_params=pltpu.CompilerParams(vmem_limit_bytes=8 * MIB),
        name=name,
    )(*arrays)


def pack_rows(arrays):
    n = sum(a.shape[0] for a in arrays)

    def body(*refs):
        planes = planes_of(refs[:-2])
        refs[-2][...] = jnp.concatenate([p[:HALO] for p in planes], axis=0)
        refs[-1][...] = jnp.concatenate([p[LAT - HALO :] for p in planes], axis=0)

    return pl.pallas_call(
        body,
        out_shape=[jax.ShapeDtypeStruct((n * HALO, LON), F32)] * 2,
        compiler_params=pltpu.CompilerParams(vmem_limit_bytes=8 * MIB),
        name="static_rows",
    )(*arrays)


def beside_lat(arrays, up, down):
    n = sum(a.shape[0] for a in arrays)

    def body(*refs):
        u_ref, w_ref, out_ref = refs[-3:]
        zero = jnp.zeros((8 - HALO, LON), F32)
        for k, plane in enumerate(planes_of(refs[:-3])):
            at = pl.ds(k * HALO, HALO)
            out_ref[k] = jnp.concatenate([zero, u_ref[at], plane, w_ref[at], zero], axis=0)

    return pl.pallas_call(
        body,
        out_shape=jax.ShapeDtypeStruct((n, PAD_LAT, LON), F32),
        compiler_params=pltpu.CompilerParams(vmem_limit_bytes=8 * MIB),
        name="static_planes",
    )(*arrays, up, down)


def side_of(k, left, right):
    lane = lax.broadcasted_iota(jnp.int32, right.shape, 1)
    to_right = (-HALO * k) % 128
    to_left = (128 - HALO - HALO * k) % 128
    right = pltpu.roll(right, to_right, 1) if to_right else right
    left = pltpu.roll(left, to_left, 1) if to_left else left
    return jnp.where(lane < HALO, right, jnp.where(lane >= 128 - HALO, left, 0.0))


def strips_of(plane):
    return [plane[8 * r : 8 * r + 8] for r in range(PAD_LAT // 8)]


def up_and_down(field):
    row = lax.broadcasted_iota(jnp.int32, field[0].shape, 0)
    before = [pltpu.roll(f, 1, 0) for f in field]
    after = [pltpu.roll(f, 7, 0) for f in field]
    last = len(field) - 1
    return [
        jnp.where(row == 0, before[max(r - 1, 0)], before[r])
        + jnp.where(row == 7, after[min(r + 1, last)], after[r])
        for r in range(len(field))
    ]


def band(c, t, taps_ref, planes, scale):
    out = []
    for r, strip in enumerate(scale):
        total = taps_ref[c, 0] * planes[t][r]
        for k in range(1, 2 * HB + 1):
            total = total + taps_ref[c, k] * planes[t + k][r]
        out.append(strip * total)
    return out


def planes_of(refs):
    return [ref[k].astype(F32) for ref in refs for k in range(ref.shape[0])]


def begin(arrays, taps):
    n = TS_DEV + 2 * HB

    def body(taps_ref, *refs):
        start_ref, part_ref = refs[-2:]
        planes = [strips_of(p) for p in planes_of(refs[:-2])]
        for c in range(TRACERS):
            for t in range(TS_DEV):
                field = band(c, t, taps_ref, planes, planes[n + c])
                for r, beside in enumerate(up_and_down(field)):
                    at = pl.ds(8 * r, 8)
                    start_ref[c, t, at] = field[r]
                    rate = planes[n + TRACERS][r]
                    part_ref[c, t, at] = field[r] + rate * (beside - 4.0 * field[r])

    return pl.pallas_call(
        body,
        in_specs=[pl.BlockSpec(memory_space=pltpu.SMEM)]
        + [pl.BlockSpec(memory_space=pltpu.VMEM)] * len(arrays),
        out_specs=[pl.BlockSpec(memory_space=pltpu.VMEM)] * 2,
        out_shape=[jax.ShapeDtypeStruct((TRACERS, TS_DEV, PAD_LAT, LON), F32)] * 2,
        compiler_params=pltpu.CompilerParams(vmem_limit_bytes=8 * MIB),
        cost_estimate=pl.CostEstimate(
            flops=32 * MIB, bytes_accessed=4 * MIB, transcendentals=0
        ),
        name="begin",
    )(taps, *arrays)


def diffuse(started, static, left, right, taps):
    n = TS_DEV + 2 * HB
    last = PAD_LAT // 8 - 1

    def body(taps_ref, start_ref, part_ref, st_ref, l_ref, r_ref, out_ref, side_ref, done_ref, sems):
        for k in range(n + TRACERS + 1):
            side_ref[k] = side_of(k, l_ref[...], r_ref[...])
        sides = [strips_of(side_ref[k]) for k in range(n + TRACERS + 1)]
        stores = [
            pltpu.make_async_copy(done_ref.at[c], out_ref.at[c], sems.at[c])
            for c in range(TRACERS)
        ]

        def wide(main, side):
            return jnp.concatenate([main, side], axis=1)

        def rate(r):
            return wide(st_ref[TRACERS, 8 * r : 8 * r + 8], sides[n + TRACERS][r])

        def along(f):
            return pltpu.roll(f, 1, 1) + pltpu.roll(f, PAD_LON - 1, 1)

        for c in range(TRACERS):
            for t in range(TS_DEV):
                side = band(c, t, taps_ref, sides, sides[n + c])
                field = []
                for r, beside in enumerate(up_and_down(side)):
                    at = pl.ds(8 * r, 8)
                    part = side[r] + sides[n + TRACERS][r] * (beside - 4.0 * side[r])
                    both = along(wide(start_ref[c, t, at], side[r]))
                    field.append(wide(part_ref[c, t, at], part) + rate(r) * both)
                for step in range(1, KSTEPS):
                    beside = up_and_down(field)
                    stepped = list(field)
                    end = step == KSTEPS - 1
                    for r in range(end, last + 1 - end):
                        total = along(field[r]) + beside[r]
                        stepped[r] = field[r] + rate(r) * (total - 4.0 * field[r])
                    field = stepped
                for r in range(1, last):
                    done_ref[c, t, 8 * r - 8 : 8 * r, :] = (
                        st_ref[c, 8 * r : 8 * r + 8] * field[r][:, :LON]
                    )
            stores[c].start()
        for store in stores:
            store.wait()

    operands = (*started, static, left, right)
    return pl.pallas_call(
        body,
        in_specs=[pl.BlockSpec(memory_space=pltpu.SMEM)]
        + [pl.BlockSpec(memory_space=pltpu.VMEM)] * len(operands),
        out_specs=pl.BlockSpec(memory_space=pl.ANY),
        out_shape=jax.ShapeDtypeStruct((TRACERS, TS_DEV, LAT, LON), F32),
        scratch_shapes=[
            pltpu.VMEM((n + TRACERS + 1, PAD_LAT, 128), F32),
            pltpu.VMEM((TRACERS, TS_DEV, LAT, LON), F32),
            pltpu.SemaphoreType.DMA((TRACERS,)),
        ],
        compiler_params=pltpu.CompilerParams(vmem_limit_bytes=12 * MIB),
        name="diffuse",
    )(taps, *operands)


def steps(axis, periodic):
    count = lax.axis_size(axis)
    forward = [(i, i + 1) for i in range(count - 1)]
    if periodic:
        forward.append((count - 1, 0))
    return forward, [(b, a) for a, b in forward]


def along_gy(parts):
    return [parts[0]] + [
        lax.ppermute(parts[k], "gy", [(i, (i + k) % N_GY) for i in range(N_GY)])
        for k in range(1, N_GY)
    ]


def along_gx(rows):
    return lax.all_to_all(rows, "gx", 0, 0, tiled=True)


def per_device(residual, footprint, tile_id, step_id, block_id, sigma, taps, diffusivity):
    east, west = steps("gx", True)
    south, north = steps("gy", False)
    later, sooner = steps("ta", False)
    ids = (tile_id[:, 0], step_id, block_id)
    first_gx, first_gy = bin_sums(ids, residual, footprint)
    got_gx = along_gx(first_gx)
    came_gy = along_gy(first_gy)

    fixed = (sigma, diffusivity[None])
    fixed, first_gy = lax.optimization_barrier((fixed, first_gy))
    to_up, to_down = pack_rows(fixed)
    up = lax.ppermute(to_down, "gy", south)
    down = lax.ppermute(to_up, "gy", north)
    came_gy, up, down = lax.optimization_barrier((came_gy, up, down))
    static = beside_lat(fixed, up, down)

    all_gx = along_gy(sum_first(got_gx))
    all_gy = along_gx(sum_arrays(came_gy))
    adj, low, high = tile_sum(all_gx, all_gy)
    before = lax.ppermute(high, "ta", later)
    after = lax.ppermute(low, "ta", sooner)
    arrays = (before, adj, after, static)
    to_left, to_right = pack_lon(arrays, F32, "halo_lon")
    left = lax.ppermute(to_right, "gx", east)
    right = lax.ppermute(to_left, "gx", west)
    return diffuse(begin(arrays, taps), static, left, right, taps)


def solution(mesh):
    return jax.shard_map(
        per_device,
        mesh=mesh,
        in_specs=(
            P(("ta", "gy", "gx")),
            P(("ta", "gy", "gx"), None),
            P(("ta", "gy", "gx"), None),
            P(("ta", "gy", "gx")),
            P(("ta", "gy", "gx")),
            P(None, "gy", "gx"),
            P(),
            P("gy", "gx"),
        ),
        out_specs=P(None, "ta", "gy", "gx"),
        check_vma=False,
    )
```

```python
import jax
import jax.numpy as jnp
from jax import lax
from jax.experimental import pallas as pl
from jax.experimental.pallas import tpu as pltpu
from jax.sharding import PartitionSpec as P

TS_DEV = 4
TRACERS = 4
HB = 2
KSTEPS = 4
LAT = 64
LON = 256
FP = 1024
HALF = FP // 2
BINS = 64
SND = 2048
N_GY = 4
N_GX = 8
TILES = N_GY * N_GX
PAD_LAT = LAT + 16
PAD_LON = LON + 128
ROWS = BINS + 16
HALO = KSTEPS
F32 = jnp.float32
BF16 = jnp.bfloat16
MIB = 1 << 20


def bin_sums(ids, residual, footprint):
    rows = N_GX * BINS
    most = BINS - 8

    def body(tile_ref, step_ref, block_ref, res_ref, fp_ref, first_ref, *refs):
        fp_buf, sel_ref, first_buf, second_buf, in_sems, first_sems, second_sems = refs[N_GY:]
        loads = [
            pltpu.make_async_copy(
                fp_ref.at[:, pl.ds(h * HALF, HALF)], fp_buf.at[h], in_sems.at[h]
            )
            for h in range(2)
        ]
        for load in loads:
            load.start()
        tile = tile_ref[...].reshape(1, SND)
        block = block_ref[...].reshape(1, SND)
        local = (block >> 1) * 8 + step_ref[...].reshape(1, SND) * 2 + (block & 1)
        away = (tile // N_GX - lax.axis_index("gy")) & (N_GY - 1)
        bins = ((away * N_GX + (tile & (N_GX - 1))) * BINS + local).astype(jnp.int16)
        weight = jnp.broadcast_to(res_ref[...].reshape(1, SND).astype(BF16), (16, SND))
        above = bins - lax.broadcasted_iota(jnp.int32, (16, SND), 0).astype(jnp.int16)

        @pl.loop(0, TILES * BINS // 16, unroll=4)
        def _(m):
            hit = above == (m * 16).astype(jnp.int16)
            sel_ref[pl.ds(pl.multiple_of(m * 16, 16), 16), :] = jnp.where(
                hit, weight, jnp.zeros((16, SND), BF16)
            )

        for load in loads:
            load.wait()
        stores = []
        for k in range(N_GY):
            halves = [
                jnp.dot(
                    sel_ref[k * rows : (k + 1) * rows, :],
                    fp_buf[h],
                    preferred_element_type=F32,
                ).reshape(N_GX, BINS, HALF)
                for h in range(2)
            ]
            for h, buf in enumerate((first_buf, second_buf)):
                both = [halves[h][:, :most], halves[1 - h][:, most:]]
                buf[k] = jnp.concatenate(both, axis=1).astype(BF16)
            stores += [
                pltpu.make_async_copy(
                    first_buf.at[k],
                    first_ref.at[:, pl.ds(k * BINS, BINS), :],
                    first_sems.at[k],
                ),
                pltpu.make_async_copy(second_buf.at[k], refs[k], second_sems.at[k]),
            ]
            stores[-2].start()
            stores[-1].start()
        for store in stores:
            store.wait()

    one = pl.BlockSpec((SND,), lambda: (0,))
    far = pl.BlockSpec(memory_space=pl.ANY)
    outs = pl.pallas_call(
        body,
        in_specs=[one] * 4 + [far],
        out_specs=[far] * (1 + N_GY),
        out_shape=[jax.ShapeDtypeStruct((N_GX, N_GY * BINS, HALF), BF16)]
        + [jax.ShapeDtypeStruct((N_GX, BINS, HALF), BF16)] * N_GY,
        scratch_shapes=[
            pltpu.VMEM((2, SND, HALF), BF16),
            pltpu.VMEM((TILES * BINS, SND), BF16),
            pltpu.VMEM((N_GY, N_GX, BINS, HALF), BF16),
            pltpu.VMEM((N_GY, N_GX, BINS, HALF), BF16),
            pltpu.SemaphoreType.DMA((2,)),
            pltpu.SemaphoreType.DMA((N_GY,)),
            pltpu.SemaphoreType.DMA((N_GY,)),
        ],
        compiler_params=pltpu.CompilerParams(vmem_limit_bytes=58 * MIB),
        cost_estimate=pl.CostEstimate(
            flops=2 * TILES * BINS * SND * FP, bytes_accessed=8 * MIB, transcendentals=0
        ),
        name="bin_sums",
    )(*ids, residual, footprint)
    return outs[0], outs[1:]


def sum_first(got):
    count, rows, cols = got.shape

    def body(got_ref, *out_refs):
        totals = []
        for k in range(N_GY):
            at = pl.ds(k * BINS, BINS)
            total = got_ref[0, at].astype(F32)
            for s in range(1, count):
                total = total + got_ref[s, at].astype(F32)
            totals.append(total)
        for k, out_ref in enumerate(out_refs):
            below = totals[(k + 1) % N_GY][:8]
            over = totals[(k - 1) % N_GY][BINS - 8 :]
            out_ref[...] = jnp.concatenate([totals[k], below, over], axis=0).astype(BF16)

    return pl.pallas_call(
        body,
        out_shape=[jax.ShapeDtypeStruct((ROWS, cols), BF16)] * N_GY,
        compiler_params=pltpu.CompilerParams(vmem_limit_bytes=12 * MIB),
        name="sum_first",
    )(got)


def sum_arrays(arrays):
    def body(*refs):
        for q in range(N_GX):
            total = refs[0][q].astype(F32)
            for ref in refs[1:-1]:
                total = total + ref[q].astype(F32)
            refs[-1][q] = total.astype(BF16)

    return pl.pallas_call(
        body,
        out_shape=jax.ShapeDtypeStruct(arrays[0].shape, BF16),
        compiler_params=pltpu.CompilerParams(vmem_limit_bytes=12 * MIB),
        name="sum_arrays",
    )(*arrays)


def tile_sum(summed, got):
    count = got.shape[0]

    def body(*refs):
        got_ref, adj_ref, low_ref, high_ref, by_row = refs[-5:]
        first = refs[0][...].astype(F32)
        for ref in refs[1:-5]:
            first = first + ref[...].astype(F32)
        last = got_ref[0].astype(F32)
        for s in range(1, count):
            last = last + got_ref[s].astype(F32)
        by_row[...] = jnp.zeros_like(by_row)

        def put(row, part, at, i):
            by_row[pl.ds(row, 8, stride=PAD_LAT), :] = part[
                at : at + 8, i * 128 : i * 128 + 128
            ]

        for i in range(4):
            for br in range(7):
                put(8 + br * 8 + i, first, br * 8, i)
                put(8 + br * 8 + 4 + i, last, br * 8, i)
            put(LAT + i, last, BINS - 8, i)
            put(LAT + 4 + i, first, BINS - 8, i)
            put(8 + LAT + i, first, BINS, i)
            put(4 + i, first, BINS + 8, i)
        for t in range(TS_DEV):
            for bc in range(2):
                at = (t * 2 + bc) * PAD_LAT
                adj_ref[t, :, bc * 128 : bc * 128 + 128] = by_row[at : at + PAD_LAT]
        low_ref[...] = adj_ref[:HB].astype(BF16)
        high_ref[...] = adj_ref[TS_DEV - HB :].astype(BF16)

    return pl.pallas_call(
        body,
        out_shape=[
            jax.ShapeDtypeStruct((TS_DEV, PAD_LAT, LON), F32),
            jax.ShapeDtypeStruct((HB, PAD_LAT, LON), BF16),
            jax.ShapeDtypeStruct((HB, PAD_LAT, LON), BF16),
        ],
        scratch_shapes=[pltpu.VMEM((TS_DEV * 2 * PAD_LAT, 128), F32)],
        compiler_params=pltpu.CompilerParams(vmem_limit_bytes=8 * MIB),
        name="tile_sum",
    )(*summed, got)


def put_strips(strip, dtype):
    rows = strip[0].shape[0]
    lane = lax.broadcasted_iota(jnp.int32, (rows, 128), 1)

    def packed(planes, side):
        out = jnp.zeros((rows, 128), F32)
        for k, plane in enumerate(planes):
            if side == 0:
                part = plane[:, :128]
                shift = HALO * k
            else:
                part = plane[:, LON - 128 :]
                shift = HALO * k + HALO
            moved = pltpu.roll(part, shift % 128, 1) if shift % 128 else part
            out = jnp.where((lane >= HALO * k) & (lane < HALO * k + HALO), moved, out)
        return out.astype(dtype)

    return packed(strip, 0), packed(strip, 1)


def pack_lon(arrays, dtype, name):
    counts = [a.shape[0] for a in arrays]

    def body(*refs):
        planes = [
            ref[k].astype(F32) for ref, count in zip(refs, counts) for k in range(count)
        ]
        refs[-2][...], refs[-1][...] = put_strips(planes, dtype)

    return pl.pallas_call(
        body,
        out_shape=[jax.ShapeDtypeStruct((arrays[0].shape[1], 128), dtype)] * 2,
        compiler_params=pltpu.CompilerParams(vmem_limit_bytes=8 * MIB),
        name=name,
    )(*arrays)


def pack_rows(arrays):
    n = sum(a.shape[0] for a in arrays)

    def body(*refs):
        planes = planes_of(refs[:-2])
        refs[-2][...] = jnp.concatenate([p[:HALO] for p in planes], axis=0)
        refs[-1][...] = jnp.concatenate([p[LAT - HALO :] for p in planes], axis=0)

    return pl.pallas_call(
        body,
        out_shape=[jax.ShapeDtypeStruct((n * HALO, LON), F32)] * 2,
        compiler_params=pltpu.CompilerParams(vmem_limit_bytes=8 * MIB),
        name="static_rows",
    )(*arrays)


def beside_lat(arrays, up, down):
    n = sum(a.shape[0] for a in arrays)

    def body(*refs):
        u_ref, w_ref, out_ref = refs[-3:]
        zero = jnp.zeros((8 - HALO, LON), F32)
        for k, plane in enumerate(planes_of(refs[:-3])):
            at = pl.ds(k * HALO, HALO)
            out_ref[k] = jnp.concatenate([zero, u_ref[at], plane, w_ref[at], zero], axis=0)

    return pl.pallas_call(
        body,
        out_shape=jax.ShapeDtypeStruct((n, PAD_LAT, LON), F32),
        compiler_params=pltpu.CompilerParams(vmem_limit_bytes=8 * MIB),
        name="static_planes",
    )(*arrays, up, down)


def side_of(k, left, right):
    lane = lax.broadcasted_iota(jnp.int32, right.shape, 1)
    to_right = (-HALO * k) % 128
    to_left = (128 - HALO - HALO * k) % 128
    right = pltpu.roll(right, to_right, 1) if to_right else right
    left = pltpu.roll(left, to_left, 1) if to_left else left
    return jnp.where(lane < HALO, right, jnp.where(lane >= 128 - HALO, left, 0.0))


def strips_of(plane):
    return [plane[8 * r : 8 * r + 8] for r in range(PAD_LAT // 8)]


def up_and_down(field):
    row = lax.broadcasted_iota(jnp.int32, field[0].shape, 0)
    before = [pltpu.roll(f, 1, 0) for f in field]
    after = [pltpu.roll(f, 7, 0) for f in field]
    last = len(field) - 1
    return [
        jnp.where(row == 0, before[max(r - 1, 0)], before[r])
        + jnp.where(row == 7, after[min(r + 1, last)], after[r])
        for r in range(len(field))
    ]


def band(c, t, taps_ref, planes, scale):
    out = []
    for r, strip in enumerate(scale):
        total = taps_ref[c, 0] * planes[t][r]
        for k in range(1, 2 * HB + 1):
            total = total + taps_ref[c, k] * planes[t + k][r]
        out.append(strip * total)
    return out


def planes_of(refs):
    return [ref[k].astype(F32) for ref in refs for k in range(ref.shape[0])]


def begin(arrays, taps):
    n = TS_DEV + 2 * HB

    def body(taps_ref, *refs):
        start_ref, part_ref = refs[-2:]
        planes = [strips_of(p) for p in planes_of(refs[:-2])]
        for c in range(TRACERS):
            for t in range(TS_DEV):
                field = band(c, t, taps_ref, planes, planes[n + c])
                for r, beside in enumerate(up_and_down(field)):
                    at = pl.ds(8 * r, 8)
                    start_ref[c, t, at] = field[r]
                    rate = planes[n + TRACERS][r]
                    part_ref[c, t, at] = field[r] + rate * (beside - 4.0 * field[r])

    return pl.pallas_call(
        body,
        in_specs=[pl.BlockSpec(memory_space=pltpu.SMEM)]
        + [pl.BlockSpec(memory_space=pltpu.VMEM)] * len(arrays),
        out_specs=[pl.BlockSpec(memory_space=pltpu.VMEM)] * 2,
        out_shape=[jax.ShapeDtypeStruct((TRACERS, TS_DEV, PAD_LAT, LON), F32)] * 2,
        compiler_params=pltpu.CompilerParams(vmem_limit_bytes=8 * MIB),
        cost_estimate=pl.CostEstimate(
            flops=32 * MIB, bytes_accessed=4 * MIB, transcendentals=0
        ),
        name="begin",
    )(taps, *arrays)


def diffuse(started, static, left, right, taps):
    n = TS_DEV + 2 * HB
    last = PAD_LAT // 8 - 1

    def body(taps_ref, start_ref, part_ref, st_ref, l_ref, r_ref, out_ref, side_ref, done_ref, sems):
        for k in range(n + TRACERS + 1):
            side_ref[k] = side_of(k, l_ref[...], r_ref[...])
        sides = [strips_of(side_ref[k]) for k in range(n + TRACERS + 1)]
        stores = [
            pltpu.make_async_copy(done_ref.at[c], out_ref.at[c], sems.at[c])
            for c in range(TRACERS)
        ]

        def wide(main, side):
            return jnp.concatenate([main, side], axis=1)

        def rate(r):
            return wide(st_ref[TRACERS, 8 * r : 8 * r + 8], sides[n + TRACERS][r])

        def along(f):
            return pltpu.roll(f, 1, 1) + pltpu.roll(f, PAD_LON - 1, 1)

        for c in range(TRACERS):
            for t in range(TS_DEV):
                side = band(c, t, taps_ref, sides, sides[n + c])
                field = []
                for r, beside in enumerate(up_and_down(side)):
                    at = pl.ds(8 * r, 8)
                    part = side[r] + sides[n + TRACERS][r] * (beside - 4.0 * side[r])
                    both = along(wide(start_ref[c, t, at], side[r]))
                    field.append(wide(part_ref[c, t, at], part) + rate(r) * both)
                for step in range(1, KSTEPS):
                    beside = up_and_down(field)
                    stepped = list(field)
                    end = step == KSTEPS - 1
                    for r in range(end, last + 1 - end):
                        total = along(field[r]) + beside[r]
                        stepped[r] = field[r] + rate(r) * (total - 4.0 * field[r])
                    field = stepped
                for r in range(1, last):
                    done_ref[c, t, 8 * r - 8 : 8 * r, :] = (
                        st_ref[c, 8 * r : 8 * r + 8] * field[r][:, :LON]
                    )
            stores[c].start()
        for store in stores:
            store.wait()

    operands = (*started, static, left, right)
    return pl.pallas_call(
        body,
        in_specs=[pl.BlockSpec(memory_space=pltpu.SMEM)]
        + [pl.BlockSpec(memory_space=pltpu.VMEM)] * len(operands),
        out_specs=pl.BlockSpec(memory_space=pl.ANY),
        out_shape=jax.ShapeDtypeStruct((TRACERS, TS_DEV, LAT, LON), F32),
        scratch_shapes=[
            pltpu.VMEM((n + TRACERS + 1, PAD_LAT, 128), F32),
            pltpu.VMEM((TRACERS, TS_DEV, LAT, LON), F32),
            pltpu.SemaphoreType.DMA((TRACERS,)),
        ],
        compiler_params=pltpu.CompilerParams(vmem_limit_bytes=12 * MIB),
        name="diffuse",
    )(taps, *operands)


def steps(axis, periodic):
    count = lax.axis_size(axis)
    forward = [(i, i + 1) for i in range(count - 1)]
    if periodic:
        forward.append((count - 1, 0))
    return forward, [(b, a) for a, b in forward]


def along_gy(parts):
    came = [parts[0]]
    for k in (2, 1, 3):
        ring = [(i, (i + k) % N_GY) for i in range(N_GY)]
        came.append(lax.ppermute(parts[k], "gy", ring))
    return came


def along_gx(rows):
    return lax.all_to_all(rows, "gx", 0, 0, tiled=True)


def per_device(residual, footprint, tile_id, step_id, block_id, sigma, taps, diffusivity):
    east, west = steps("gx", True)
    south, north = steps("gy", False)
    later, sooner = steps("ta", False)
    ids = (tile_id[:, 0], step_id, block_id)
    first_gx, first_gy = bin_sums(ids, residual, footprint)
    got_gx = along_gx(first_gx)
    came_gy = along_gy(first_gy)

    fixed = (sigma, diffusivity[None])
    fixed, first_gy = lax.optimization_barrier((fixed, first_gy))
    to_up, to_down = pack_rows(fixed)
    up = lax.ppermute(to_down, "gy", south)
    down = lax.ppermute(to_up, "gy", north)
    came_gy, up, down = lax.optimization_barrier((came_gy, up, down))
    static = beside_lat(fixed, up, down)

    all_gx = along_gy(sum_first(got_gx))
    all_gy = along_gx(sum_arrays(came_gy))
    adj, low, high = tile_sum(all_gx, all_gy)
    before = lax.ppermute(high, "ta", later)
    after = lax.ppermute(low, "ta", sooner)
    arrays = (before, adj, after, static)
    to_left, to_right = pack_lon(arrays, F32, "halo_lon")
    left = lax.ppermute(to_right, "gx", east)
    right = lax.ppermute(to_left, "gx", west)
    return diffuse(begin(arrays, taps), static, left, right, taps)


def solution(mesh):
    return jax.shard_map(
        per_device,
        mesh=mesh,
        in_specs=(
            P(("ta", "gy", "gx")),
            P(("ta", "gy", "gx"), None),
            P(("ta", "gy", "gx"), None),
            P(("ta", "gy", "gx")),
            P(("ta", "gy", "gx")),
            P(None, "gy", "gx"),
            P(),
            P("gy", "gx"),
        ),
        out_specs=P(None, "ta", "gy", "gx"),
        check_vma=False,
    )
```
